32 devices in a mesh: lat: 8 (over y, x, core), lon: 4 (over z).
Axes of the slice: x: 2, y: 2, z: 4, core: 2. Of those that a mesh axis runs over, the one named last changes fastest.
Arguments:
- tracer: float32 [32, 256, 2048], P(None, 'lat', 'lon'), may hold values from -6 to 6
- source: int32 [256, 16], P('lat', 'lon'), may hold values from 0 to 4095, as said below
- offset: int32 [256, 2048], P('lat', 'lon'), may hold values from 1 to 125
- fraction: float32 [256, 2048], P('lat', 'lon'), may hold values from 0 to 1
- cutoffs: int32 [2, 8], replicated, may hold values from 2 to 255
Outputs:
- advected: float32 [32, 256, 2048], P(None, 'lat', 'lon')
The draws below stay inside these ranges and needn't reach their ends.
Inputs may be any that keep to these rules, and one draw needn't show every extreme that they name: With source[j, b] = rho * 16 + beta: |rho - j| <= 2, and some arrival blocks reach 2 in both directions. Rows j with 8 <= j < 248 have beta equal to b - 1, b or b + 1 modulo 16. Rows within 8 of a pole have rho within the same band of 8 rows at that pole and beta anywhere on the circle.
All inputs are finite; a program needn't handle non-finite values.
Results may differ from the reference program's by a relative error of at most 0.000071.
Values sent between devices are 32-bit elements; how exact they have to be, the bound alone decides.
A program may use at most 128 MiB of HBM per device.

```python
import jax
import jax.numpy as jnp
from jax import lax

NLON = 2048
BLK = 128
HL = 2
PROWS = 8
C = 32
NLAT = 256
NBLK = 16


def draw_source(key, part):
    row_key, step_key = jax.random.split(jax.random.fold_in(key, 17), 2)
    row_ids = jnp.arange(NLAT, dtype=jnp.int32)[:, None]
    blocks = jnp.arange(NBLK, dtype=jnp.int32)[None, :]
    row_step = jax.random.randint(row_key, (NLAT, NBLK), -HL, HL + 1)
    serial = row_ids * NBLK + blocks
    row_step = jnp.where(serial % 97 == 5, HL, row_step)
    row_step = jnp.where(serial % 97 == 11, -HL, row_step)
    pole_distance = jnp.minimum(row_ids, NLAT - 1 - row_ids)
    near_pole = pole_distance < PROWS
    northern = row_ids < NLAT // 2
    lowest_row = jnp.where(near_pole & jnp.logical_not(northern), NLAT - PROWS, 0)
    highest_row = jnp.where(near_pole & northern, PROWS - 1, NLAT - 1)
    start_row = jnp.clip(row_ids + row_step, lowest_row, highest_row)
    block_reach = jnp.where(near_pole, 1 + (NBLK // 2 - 1) * (PROWS - pole_distance) // PROWS, 1)
    random_bits = jax.random.randint(step_key, (NLAT, NBLK), 0, 1 << 20)
    block_shift = random_bits % (2 * block_reach + 1) - block_reach
    start_block = jnp.mod(blocks + block_shift, NBLK)
    return (start_row * NBLK + start_block).astype(jnp.int32)


def with_ends(values, stream_key, least, top_value):
    dims = values.shape
    spot = [jax.random.randint(jax.random.fold_in(stream_key, axis), (), 0, dims[axis]) for axis in range(len(dims))]
    values = values.at[tuple(spot)].set(least)
    longest = dims.index(max(dims))
    spot[longest] = (spot[longest] + 1) % dims[longest]
    return values.at[tuple(spot)].set(top_value)


def levels(stream_key, dims, cuts, low, top_value):
    factor_of, own = 1.0, jax.random.fold_in(stream_key, 6)
    for axis_at, blocks in cuts:
        heights = jnp.exp(jax.random.uniform(jax.random.fold_in(own, axis_at), (blocks,), jnp.float32, low / len(cuts), top_value / len(cuts)))
        factor_of = factor_of * jnp.repeat(heights, dims[axis_at] // blocks).reshape([-1 if axis == axis_at else 1 for axis in range(len(dims))])
    return factor_of


def scatter_about(rng, shape, deviation, limit, cuts=(), kind=jnp.bfloat16):
    drawn = deviation * jax.random.normal(rng, shape, jnp.float32)
    if cuts:
        drawn = drawn * levels(rng, shape, cuts, -0.22, 0.18)
    return jnp.clip(drawn, -limit, limit).astype(kind)


def setup_inputs(seed: int = 0) -> dict:
    keys = jax.random.split(jax.random.key(seed), 6)
    return {
        "tracer": scatter_about(keys[0], (C, NLAT, NLON), 1.0, 6.0, ((1, 8), (2, 4)), jnp.float32),
        "source": draw_source(jax.random.fold_in(keys[5], 71), 0),
        "offset": with_ends(jax.random.randint(keys[2], (NLAT, NLON), 1, BLK - 2), jax.random.fold_in(keys[2], 1), 1, (BLK - 2) - 1).astype(jnp.int32),
        "fraction": jnp.clip(1.0 * jax.random.uniform(keys[3], (NLAT, NLON), jnp.float32) ** levels(keys[3], (NLAT, NLON), ((0, 8), (1, 4)), -0.2, 0.2), 0.0, 1.0),
        "cutoffs": with_ends(jax.random.randint(keys[4], (2, PROWS), 2, NLON // 8), jax.random.fold_in(keys[4], 1), 2, (NLON // 8) - 1).astype(jnp.int32),
    }


def cubic_limited(before_one, at_anchor, after_one, after_two, position):
    weight_before = -position * (position - 1.0) * (position - 2.0) / 6.0
    weight_anchor = (position + 1.0) * (position - 1.0) * (position - 2.0) / 2.0
    weight_after = -(position + 1.0) * position * (position - 2.0) / 2.0
    weight_beyond = (position + 1.0) * position * (position - 1.0) / 6.0
    interpolated = weight_before * before_one + weight_anchor * at_anchor + weight_after * after_one + weight_beyond * after_two
    lowest_bound = jnp.minimum(at_anchor, after_one)
    upper_bound = jnp.maximum(at_anchor, after_one)
    return jnp.minimum(jnp.maximum(interpolated, lowest_bound), upper_bound)


def reference(tracer, source, offset, fraction, cutoffs):
    cell_ids = jnp.arange(NLON, dtype=jnp.int32)
    per_cell = jnp.take(source, cell_ids // BLK, axis=1)
    source_row = per_cell // NBLK
    source_block = per_cell % NBLK
    anchor = (source_row * NLON + source_block * BLK + offset).astype(jnp.int32)
    polar_rows = jnp.concatenate([jnp.arange(PROWS, dtype=jnp.int32), NLAT - PROWS + jnp.arange(PROWS, dtype=jnp.int32)])
    wavenumbers = jnp.arange(NLON // 2 + 1, dtype=jnp.int32)
    cutoff_values = cutoffs.reshape(2 * PROWS).astype(jnp.float32)
    ratios = cutoff_values[:, None] / jnp.maximum(wavenumbers, 1).astype(jnp.float32)[None, :]
    inside = (wavenumbers >= 1) & (wavenumbers < NLON // 2)
    damping = jnp.where(inside[None, :], jnp.maximum(1.0 - ratios, 0.0), 0.0)

    def advect(channel_field):
        flat_values = channel_field.reshape(-1)
        limited = cubic_limited(flat_values[anchor - 1], flat_values[anchor], flat_values[anchor + 1], flat_values[anchor + 2], fraction)
        polar_band = limited[polar_rows]
        spectrum = jnp.fft.rfft(polar_band, axis=-1)
        removed = jnp.fft.irfft(spectrum * damping, n=NLON, axis=-1)
        return limited.at[polar_rows].set(polar_band - removed.astype(polar_band.dtype))

    return lax.map(advect, tracer)
```

```python
import functools
import math

import jax
import jax.numpy as jnp
import numpy as np
from jax import lax
from jax.experimental import pallas as pl
from jax.experimental.pallas import tpu as pltpu
from jax.sharding import PartitionSpec as P

NLON = 2048
BLK = 128
HL = 2
PROWS = 8
NBLK = NLON // BLK
SUB = 8
HALF = NBLK // 2 + 1
MESH = pl.DeviceIdType.MESH


def dft_tables():
    lanes = np.arange(BLK)
    angles = 2.0 * math.pi * (np.outer(lanes, lanes) % BLK) / BLK
    cosines, sines = np.cos(angles), np.sin(angles)
    matrix = np.block([[cosines, -sines], [sines, cosines]])
    turns = 2.0 * math.pi * np.outer(np.arange(NBLK), lanes) / NLON
    twiddle = np.stack([np.cos(turns), np.sin(turns)])
    return matrix.astype(np.float32), twiddle.astype(np.float32)


def add(left, right):
    if left is None:
        return right
    return left if right is None else left + right


def sub(left, right):
    if right is None:
        return left
    return -right if left is None else left - right


def scaled(value, factor):
    return None if value is None or factor == 0.0 else value * factor


def turned(value, cosine, sine):
    re, im = value
    cosine, sine = (0.0 if abs(v) < 1e-12 else v for v in (cosine, sine))
    if sine == 0.0 and cosine == 1.0:
        return value
    if cosine == 0.0 and abs(sine) == 1.0:
        if sine > 0:
            return (None if im is None else -im), re
        return im, (None if re is None else -re)
    return sub(scaled(re, cosine), scaled(im, sine)), add(scaled(re, sine), scaled(im, cosine))


def fourier(values, sign):
    count = len(values)
    if count == 1:
        return values
    even, odd = fourier(values[::2], sign), fourier(values[1::2], sign)
    low, high = [], []
    for k in range(count // 2):
        angle = sign * 2.0 * math.pi * k / count
        re, im = turned(odd[k], math.cos(angle), math.sin(angle))
        low.append((add(even[k][0], re), add(even[k][1], im)))
        high.append((sub(even[k][0], re), sub(even[k][1], im)))
    return low + high


def weights_of(t):
    return (
        -t * (t - 1.0) * (t - 2.0) / 6.0,
        (t + 1.0) * (t - 1.0) * (t - 2.0) / 2.0,
        -(t + 1.0) * t * (t - 2.0) / 2.0,
        (t + 1.0) * t * (t - 1.0) / 6.0,
    )


def wide(row):
    return jnp.broadcast_to(row, (SUB, BLK))


def lanes_at(values, index):
    return jnp.take_along_axis(values, index, axis=1, mode="promise_in_bounds")


def row_of(values, row):
    index = jnp.full((SUB, BLK), row, jnp.int32)
    return jnp.take_along_axis(values, index, axis=0, mode="promise_in_bounds")


def cubic_limited(values, anchor, weights):
    before = lanes_at(values, anchor - 1)
    here = lanes_at(values, anchor)
    after = lanes_at(values, anchor + 1)
    beyond = lanes_at(values, anchor + 2)
    mixed = weights[0] * before + weights[1] * here + weights[2] * after + weights[3] * beyond
    return jnp.minimum(jnp.maximum(mixed, jnp.minimum(here, after)), jnp.maximum(here, after))


def lanes(block):
    return pl.ds(pl.multiple_of(block * BLK, BLK), BLK)


def kernel(
    n_lat, n_lon, src_s, cut_s, trc, src_v, off, frac, mat, twd, out,
    mid, side, ring, ids, ids_out, fracs, ids_s, lim, spec, done, back,
    halo_send, halo_recv, pol_send, pol_recv, idx_send, idx_recv, frc_send, frc_recv,
    ret_send, ret_recv, loc_sem,
):
    channels, rows, cells = trc.shape
    nb = cells // BLK
    groups = channels // SUB
    shares = n_lon // groups
    work_rows = PROWS // shares
    tall = work_rows * SUB
    lat, lon = lax.axis_index("lat"), lax.axis_index("lon")
    first_row = lat * rows
    first_block = lon * nb
    right, left = lax.rem(lon + 1, n_lon), lax.rem(lon + n_lon - 1, n_lon)
    down, up = lax.rem(lat + 1, n_lat), lax.rem(lat + n_lat - 1, n_lat)
    polar = (lat == 0) | (lat == n_lat - 1)
    slab = jnp.where(lat == 0, 0, rows - PROWS)
    peers = [lax.rem(lon + d, n_lon) for d in range(1, n_lon)]

    barrier = pltpu.get_barrier_semaphore()
    for peer in peers:
        pl.semaphore_signal(barrier, inc=1, device_id=(lat, peer), device_id_type=MESH)
    for row in (up, down):
        for col in (left, lon, right):
            pl.semaphore_signal(barrier, inc=1, device_id=(row, col), device_id_type=MESH)

    @pl.loop(0, groups * (rows // SUB))
    def _(step):
        ch = pl.multiple_of(lax.rem(step, groups) * SUB, SUB)
        row = pl.multiple_of(lax.div(step, groups) * SUB, SUB)
        for b in range(nb):
            tile = trc[pl.ds(ch, SUB), pl.ds(row, SUB), b * BLK : (b + 1) * BLK]
            mid[pl.ds(HL + row, SUB), b, pl.ds(ch, SUB), :] = jnp.swapaxes(tile, 0, 1)

    pl.semaphore_wait(barrier, n_lon - 1 + 6)

    def group_of(place):
        return pl.multiple_of(lax.rem(place, groups) * SUB, SUB)

    def span_of(place):
        return pl.ds(place * nb, nb)

    def remote(src, dst, send, recv, device):
        return pltpu.make_async_remote_copy(
            src_ref=src, dst_ref=dst, send_sem=send, recv_sem=recv,
            device_id=device, device_id_type=MESH,
        )

    slab_at = pl.ds(pl.multiple_of(slab, SUB), PROWS)
    own = span_of(lon)
    ring_copies, back_copies = [], []
    for d, peer in enumerate(peers):
        ring_copies += [
            remote(ids_out, ids.at[lon], idx_send.at[d], idx_recv.at[d], (lat, peer)),
            remote(frac.at[slab_at], fracs.at[lon], frc_send.at[d], frc_recv.at[d], (lat, peer)),
            remote(
                mid.at[pl.ds(HL + slab, PROWS), :, pl.ds(group_of(peer), SUB), :],
                ring.at[:, own],
                pol_send.at[d], pol_recv.at[d], (lat, peer),
            ),
        ]
        back_copies.append(
            remote(
                done.at[:, span_of(peer)],
                back.at[
                    pl.ds(lax.div(lon, groups) * work_rows, work_rows), :, pl.ds(group_of(lon), SUB), :
                ],
                ret_send.at[d], ret_recv.at[d], (lat, peer),
            )
        )

    first, last = 0, nb - 1
    inner, top, bottom = pl.ds(HL, rows), pl.ds(HL, HL), pl.ds(rows, HL)
    over, under = pl.ds(0, HL), pl.ds(HL + rows, HL)
    plan = [
        (mid.at[bottom], mid.at[over], (down, lon)),
        (mid.at[top], mid.at[under], (up, lon)),
        (mid.at[inner, last], side.at[0, inner], (lat, right)),
        (mid.at[inner, first], side.at[1, inner], (lat, left)),
        (mid.at[bottom, last], side.at[0, over], (down, right)),
        (mid.at[bottom, first], side.at[1, over], (down, left)),
        (mid.at[top, last], side.at[0, under], (up, right)),
        (mid.at[top, first], side.at[1, under], (up, left)),
    ]
    halos = [
        remote(src, dst, halo_send.at[n], halo_recv.at[n], device)
        for n, (src, dst, device) in enumerate(plan)
    ]

    @pl.when(polar)
    def _():
        ids_out[0:PROWS] = off[slab_at]
        ids_out[PROWS : 2 * PROWS] = jnp.zeros((PROWS, cells), jnp.int32)
        ids_out[PROWS : 2 * PROWS, 0:nb] = src_v[slab_at]
        for copy in ring_copies:
            copy.start()

    for copy in halos:
        copy.start()

    def tile(group, b, edge):
        row = pl.multiple_of(group * SUB, SUB)
        at = lanes(b)
        weights = weights_of(frac[pl.ds(row, SUB), at])
        anchors = off[pl.ds(row, SUB), at]
        results = [[] for _ in range(groups)]
        for j in range(SUB):
            block_id = src_s[row + j, b]
            source_row = lax.div(block_id, NBLK) - first_row + HL
            source_row = jnp.clip(source_row, 0, rows + 2 * HL - 1)
            place = lax.rem(lax.rem(block_id, NBLK) - first_block + 1 + NBLK, NBLK)
            near = jnp.clip(place - 1, 0, nb - 1)
            far = jnp.minimum(place, 1)
            spot = jnp.full((SUB, BLK), place, jnp.int32)
            inside = (spot >= 1) & (spot <= nb)
            anchor = wide(anchors[j : j + 1])
            factors = [wide(w[j : j + 1]) for w in weights]
            for g in range(groups):
                chans = pl.ds(g * SUB, SUB)
                values = mid[source_row, near, chans, :]
                if edge:
                    values = jnp.where(inside, values, side[far, source_row, chans, :])
                results[g].append(cubic_limited(values, anchor, factors))
        for g in range(groups):
            out[g * SUB : (g + 1) * SUB, pl.ds(row, SUB), at] = jnp.swapaxes(
                jnp.stack(results[g]), 0, 1
            )

    tiles = rows // SUB

    def sweep(blocks, edge):
        count = len(blocks)
        if not count:
            return
        start, stride = blocks[0], (blocks[1] - blocks[0] if count > 1 else 1)

        @pl.loop(0, tiles * count)
        def _(step):
            group = lax.div(step, count)
            at_pole = ((lat == 0) & (group == 0)) | ((lat == n_lat - 1) & (group == tiles - 1))

            @pl.when(jnp.logical_not(at_pole))
            def _():
                tile(group, start + stride * lax.rem(step, count), edge)

    @pl.when(polar)
    def _():
        ids[lon] = ids_out[...]
        fracs[lon] = frac[slab_at]
        ring[:, own] = mid[pl.ds(HL + slab, PROWS), :, pl.ds(group_of(lon), SUB), :]
        for copy in ring_copies:
            copy.wait_recv()
        fetch = pltpu.make_async_copy(
            ids.at[:, pl.ds(PROWS, PROWS), pl.ds(0, BLK)], ids_s, loc_sem.at[0]
        )
        fetch.start()
        fetch.wait()
        row_base = lax.div(lon, groups) * work_rows
        slab_global = first_row + slab
        pole = jnp.where(lat == 0, 0, 1)

        @pl.loop(0, work_rows)
        def _(j):
            jw = row_base + j
            band = []
            for b in range(NBLK):
                q, bb = b // nb, b % nb
                block_id = ids_s[q, jw, bb]
                source_row = jnp.clip(lax.div(block_id, NBLK) - slab_global, 0, PROWS - 1)
                values = ring[source_row, lax.rem(block_id, NBLK)]
                at = pl.ds(bb * BLK, BLK)
                weights = weights_of(row_of(fracs[q, :, at], jw))
                anchor = row_of(ids[q, 0:PROWS, at], jw)
                limited = cubic_limited(values, anchor, weights)
                lim[j, b] = limited
                band.append((limited, None))
            waves = fourier(band, -1)
            for k in range(HALF):
                re, im = waves[k]
                cosine, sine = wide(twd[0, k : k + 1, :]), wide(twd[1, k : k + 1, :])
                at = pl.ds(pl.multiple_of(k * tall + j * SUB, SUB), SUB)
                if im is None:
                    spec[at, 0:BLK] = re * cosine
                    spec[at, BLK : 2 * BLK] = -re * sine
                else:
                    spec[at, 0:BLK] = re * cosine + im * sine
                    spec[at, BLK : 2 * BLK] = im * cosine - re * sine

        def transform():
            spec[...] = jnp.dot(
                spec[...], mat[...], precision=lax.Precision.HIGHEST,
                preferred_element_type=jnp.float32,
            )

        transform()

        @pl.loop(0, work_rows)
        def _(j):
            kappa = cut_s[pole, row_base + j].astype(jnp.float32)
            for k in range(HALF):
                wave = k + NBLK * lax.broadcasted_iota(jnp.int32, (SUB, BLK), 1)
                wave = jnp.minimum(wave, NLON - wave)
                kept = (wave >= 1) & (wave < NLON // 2)
                damping = 1.0 - kappa / jnp.maximum(wave, 1).astype(jnp.float32)
                damping = jnp.where(kept, jnp.maximum(damping, 0.0), 0.0) * (1.0 / NLON)
                at = pl.ds(pl.multiple_of(k * tall + j * SUB, SUB), SUB)
                spec[at, 0:BLK] = spec[at, 0:BLK] * damping
                spec[at, BLK : 2 * BLK] = -spec[at, BLK : 2 * BLK] * damping

        transform()

        @pl.loop(0, work_rows)
        def _(j):
            waves = []
            for k in range(HALF):
                at = pl.ds(pl.multiple_of(k * tall + j * SUB, SUB), SUB)
                re, im = spec[at, 0:BLK], spec[at, BLK : 2 * BLK]
                cosine, sine = wide(twd[0, k : k + 1, :]), wide(twd[1, k : k + 1, :])
                real = re * cosine + im * sine
                waves.append((real, None if k in (0, HALF - 1) else re * sine - im * cosine))
            for k in range(HALF, NBLK):
                re, im = waves[NBLK - k]
                waves.append((re, -im))
            removed = fourier(waves, 1)
            for b in range(NBLK):
                done[j, b] = lim[j, b] - removed[b][0]

        for copy in back_copies:
            copy.start()
        back[pl.ds(row_base, work_rows), :, pl.ds(group_of(lon), SUB), :] = done[:, own]

    for copy in halos[:2]:
        copy.wait_recv()
    sweep(list(range(1, nb - 1)), False)
    for copy in halos[2:]:
        copy.wait_recv()
    sweep(sorted({0, nb - 1}), True)

    @pl.when(polar)
    def _():
        for copy in back_copies:
            copy.wait_recv()

        @pl.loop(0, groups)
        def _(g):
            ch = pl.multiple_of(g * SUB, SUB)
            for b in range(nb):
                at = slice(b * BLK, (b + 1) * BLK)
                out[pl.ds(ch, SUB), slab_at, at] = jnp.swapaxes(back[:, b, pl.ds(ch, SUB), :], 0, 1)

        for copy in ring_copies + back_copies:
            copy.wait_send()

    for copy in halos:
        copy.wait_send()


def body(n_lat, n_lon, tracer, source, offset, fraction, cutoffs):
    channels, rows, cells = tracer.shape
    shares = n_lon // (channels // SUB)
    work_rows = PROWS // shares
    matrix, twiddle = dft_tables()
    dma = pltpu.SemaphoreType.DMA
    vmem, smem = pl.BlockSpec(memory_space=pltpu.VMEM), pl.BlockSpec(memory_space=pltpu.SMEM)
    return pl.pallas_call(
        functools.partial(kernel, n_lat, n_lon),
        out_shape=jax.ShapeDtypeStruct(tracer.shape, jnp.float32),
        in_specs=[smem, smem] + [vmem] * 6,
        out_specs=vmem,
        scratch_shapes=[
            pltpu.VMEM((rows + 2 * HL, cells // BLK, channels, BLK), jnp.float32),
            pltpu.VMEM((2, rows + 2 * HL, channels, BLK), jnp.float32),
            pltpu.VMEM((PROWS, NBLK, SUB, BLK), jnp.float32),
            pltpu.VMEM((n_lon, 2 * PROWS, cells), jnp.int32),
            pltpu.VMEM((2 * PROWS, cells), jnp.int32),
            pltpu.VMEM((n_lon, PROWS, cells), jnp.float32),
            pltpu.SMEM((n_lon, PROWS, BLK), jnp.int32),
            pltpu.VMEM((work_rows, NBLK, SUB, BLK), jnp.float32),
            pltpu.VMEM((HALF * work_rows * SUB, 2 * BLK), jnp.float32),
            pltpu.VMEM((work_rows, NBLK, SUB, BLK), jnp.float32),
            pltpu.VMEM((PROWS, cells // BLK, channels, BLK), jnp.float32),
            dma((8,)), dma((8,)),
        ] + [dma((n_lon - 1,))] * 8 + [dma((1,))],
        compiler_params=pltpu.CompilerParams(
            collective_id=0, has_side_effects=True, vmem_limit_bytes=40 * 2**20
        ),
        cost_estimate=pl.CostEstimate(flops=10**9, bytes_accessed=5 * 10**6, transcendentals=0),
    )(source, cutoffs, tracer, source, offset, fraction, jnp.asarray(matrix), jnp.asarray(twiddle))


def solution(mesh):
    placed = (P(None, "lat", "lon"), P("lat", "lon"), P("lat", "lon"), P("lat", "lon"), P())
    step = functools.partial(body, mesh.shape["lat"], mesh.shape["lon"])
    return jax.shard_map(
        step, mesh=mesh, in_specs=placed, out_specs=P(None, "lat", "lon"), check_vma=False
    )
```

```python
import functools
import math

import jax
import jax.numpy as jnp
import numpy as np
from jax import lax
from jax.experimental import pallas as pl
from jax.experimental.pallas import tpu as pltpu
from jax.sharding import PartitionSpec as P

NLON = 2048
BLK = 128
HL = 2
PROWS = 8
NBLK = NLON // BLK
SUB = 8
HALF = NBLK // 2 + 1
MESH = pl.DeviceIdType.MESH


def dft_tables():
    lanes = np.arange(BLK)
    angles = 2.0 * math.pi * (np.outer(lanes, lanes) % BLK) / BLK
    cosines, sines = np.cos(angles), np.sin(angles)
    matrix = np.block([[cosines, -sines], [sines, cosines]])
    turns = 2.0 * math.pi * np.outer(np.arange(NBLK), lanes) / NLON
    twiddle = np.stack([np.cos(turns), np.sin(turns)])
    return matrix.astype(np.float32), twiddle.astype(np.float32)


def add(left, right):
    if left is None:
        return right
    return left if right is None else left + right


def sub(left, right):
    if right is None:
        return left
    return -right if left is None else left - right


def scaled(value, factor):
    return None if value is None or factor == 0.0 else value * factor


def turned(value, cosine, sine):
    re, im = value
    cosine, sine = (0.0 if abs(v) < 1e-12 else v for v in (cosine, sine))
    if sine == 0.0 and cosine == 1.0:
        return value
    if cosine == 0.0 and abs(sine) == 1.0:
        if sine > 0:
            return (None if im is None else -im), re
        return im, (None if re is None else -re)
    return sub(scaled(re, cosine), scaled(im, sine)), add(scaled(re, sine), scaled(im, cosine))


def fourier(values, sign):
    count = len(values)
    if count == 1:
        return values
    even, odd = fourier(values[::2], sign), fourier(values[1::2], sign)
    low, high = [], []
    for k in range(count // 2):
        angle = sign * 2.0 * math.pi * k / count
        re, im = turned(odd[k], math.cos(angle), math.sin(angle))
        low.append((add(even[k][0], re), add(even[k][1], im)))
        high.append((sub(even[k][0], re), sub(even[k][1], im)))
    return low + high


def weights_of(t):
    return (
        -t * (t - 1.0) * (t - 2.0) / 6.0,
        (t + 1.0) * (t - 1.0) * (t - 2.0) / 2.0,
        -(t + 1.0) * t * (t - 2.0) / 2.0,
        (t + 1.0) * t * (t - 1.0) / 6.0,
    )


def wide(row):
    return jnp.broadcast_to(row, (SUB, BLK))


def lanes_at(values, index):
    return jnp.take_along_axis(values, index, axis=1, mode="promise_in_bounds")


def row_of(values, row):
    index = jnp.full((SUB, BLK), row, jnp.int32)
    return jnp.take_along_axis(values, index, axis=0, mode="promise_in_bounds")


def cubic_limited(values, anchor, weights):
    before = lanes_at(values, anchor - 1)
    here = lanes_at(values, anchor)
    after = lanes_at(values, anchor + 1)
    beyond = lanes_at(values, anchor + 2)
    mixed = weights[0] * before + weights[1] * here + weights[2] * after + weights[3] * beyond
    return jnp.minimum(jnp.maximum(mixed, jnp.minimum(here, after)), jnp.maximum(here, after))


def lanes(block):
    return pl.ds(pl.multiple_of(block * BLK, BLK), BLK)


def kernel(
    n_lat, n_lon, src_h, cut_h, trc_h, off_h, frac_h, mat_h, twd_h, out,
    src_s, cut_s, trc, off, frac, mat, twd,
    mid, side_0, side_1, side_2, side_3, ring, ids, ids_out, fracs, ids_s, lim, spec, done, back,
    halo_send, halo_recv, pol_send, pol_recv, idx_send, idx_recv, frc_send, frc_recv,
    ret_send, ret_recv, loc_sem,
):
    sides = (side_0, side_1, side_2, side_3)
    channels, rows, cells = trc.shape
    nb = cells // BLK
    groups = channels // SUB
    shares = n_lon // groups
    work_rows = PROWS // shares
    tall = work_rows * SUB
    lat, lon = lax.axis_index("lat"), lax.axis_index("lon")
    first_row = lat * rows
    first_block = lon * nb
    right, left = lax.rem(lon + 1, n_lon), lax.rem(lon + n_lon - 1, n_lon)
    down, up = lax.rem(lat + 1, n_lat), lax.rem(lat + n_lat - 1, n_lat)
    polar = (lat == 0) | (lat == n_lat - 1)
    slab = jnp.where(lat == 0, 0, rows - PROWS)
    peers = [lax.rem(lon + d, n_lon) for d in range(1, n_lon)]

    edges = sorted({0, nb - 1})
    middle = list(range(1, nb - 1))

    def local(src, dst, sem):
        return pltpu.make_async_copy(src, dst, loc_sem.at[sem])

    def block_span(first_block_in, count):
        return pl.ds(first_block_in * BLK, count * BLK)

    loads = [
        local(trc_h.at[:, :, block_span(b, 1)], trc.at[:, :, block_span(b, 1)], n)
        for n, b in enumerate(edges)
    ]
    small = [local(off_h, off, 2), local(frac_h, frac, 3), local(src_h, src_s, 4)]
    tables = [local(cut_h, cut_s, 5), local(mat_h, mat, 6), local(twd_h, twd, 7)]
    for copy in loads:
        copy.start()
    centre = []
    if middle:
        span = block_span(1, len(middle))
        centre = [local(trc_h.at[:, :, span], trc.at[:, :, span], 8)]
    for copy in small + centre:
        copy.start()

    @pl.when(polar)
    def _():
        for copy in tables:
            copy.start()

    barrier = pltpu.get_barrier_semaphore()
    for peer in peers:
        pl.semaphore_signal(barrier, inc=1, device_id=(lat, peer), device_id_type=MESH)
    for row in (up, down):
        for col in (left, lon, right):
            pl.semaphore_signal(barrier, inc=1, device_id=(row, col), device_id_type=MESH)

    def turn(blocks):
        @pl.loop(0, groups * (rows // SUB))
        def _(step):
            ch = pl.multiple_of(lax.rem(step, groups) * SUB, SUB)
            row = pl.multiple_of(lax.div(step, groups) * SUB, SUB)
            for b in blocks:
                tile = trc[pl.ds(ch, SUB), pl.ds(row, SUB), b * BLK : (b + 1) * BLK]
                mid[pl.ds(HL + row, SUB), b, pl.ds(ch, SUB), :] = jnp.swapaxes(tile, 0, 1)

    for copy in loads:
        copy.wait()
    turn(edges)

    pl.semaphore_wait(barrier, n_lon - 1 + 6)

    def group_of(place):
        return pl.multiple_of(lax.rem(place, groups) * SUB, SUB)

    def span_of(place):
        return pl.ds(place * nb, nb)

    def remote(src, dst, send, recv, device):
        return pltpu.make_async_remote_copy(
            src_ref=src, dst_ref=dst, send_sem=send, recv_sem=recv,
            device_id=device, device_id_type=MESH,
        )

    slab_at = pl.ds(pl.multiple_of(slab, SUB), PROWS)
    own = span_of(lon)
    ring_copies, back_copies = [], []
    for d, peer in enumerate(peers):
        ring_copies += [
            remote(ids_out, ids.at[lon], idx_send.at[d], idx_recv.at[d], (lat, peer)),
            remote(frac.at[slab_at], fracs.at[lon], frc_send.at[d], frc_recv.at[d], (lat, peer)),
            remote(
                mid.at[pl.ds(HL + slab, PROWS), :, pl.ds(group_of(peer), SUB), :],
                ring.at[:, own],
                pol_send.at[d], pol_recv.at[d], (lat, peer),
            ),
        ]
        back_copies.append(
            remote(
                done.at[:, span_of(peer)],
                back.at[
                    pl.ds(lax.div(lon, groups) * work_rows, work_rows), :, pl.ds(group_of(lon), SUB), :
                ],
                ret_send.at[d], ret_recv.at[d], (lat, peer),
            )
        )

    first, last = 0, nb - 1
    inner, top, bottom = pl.ds(HL, rows), pl.ds(HL, HL), pl.ds(rows, HL)
    over, under = pl.ds(0, HL), pl.ds(HL + rows, HL)
    kept = rows - PROWS + HL
    some = pl.ds(HL + jnp.where(lat == 0, PROWS - HL, 0), kept)
    has_up, has_down = lat > 0, lat < n_lat - 1
    counter = iter(range(100))

    def halo(src, dst, device):
        n = next(counter)
        return remote(src, dst, halo_send.at[n], halo_recv.at[n], device)

    lat_halos = [
        (has_down, has_up, halo(mid.at[bottom], mid.at[over], (down, lon))),
        (has_up, has_down, halo(mid.at[top], mid.at[under], (up, lon))),
    ]
    lon_halos = []
    for g in range(groups):
        chans, side = pl.ds(g * SUB, SUB), sides[g]
        copies = []
        for to, block, half in ((right, last, 0), (left, first, 1)):
            n = next(counter)
            for span, when in ((inner, jnp.logical_not(polar)), (some, polar)):
                copies.append((when, when, remote(
                    mid.at[span, block, chans], side.at[half, span],
                    halo_send.at[n], halo_recv.at[n], (lat, to),
                )))
            copies.append((has_down, has_up, halo(
                mid.at[bottom, block, chans], side.at[half, over], (down, to))))
            copies.append((has_up, has_down, halo(
                mid.at[top, block, chans], side.at[half, under], (up, to))))
        lon_halos.append(copies)

    def gated(condition, action):
        @pl.when(condition)
        def _():
            action()

    for copy in small:
        copy.wait()

    @pl.when(polar)
    def _():
        for copy in centre:
            copy.wait()
        if middle:
            turn(middle)
        ids_out[0:PROWS] = off[slab_at]
        placed = jnp.zeros((PROWS, BLK), jnp.int32)
        row_ids = lax.broadcasted_iota(jnp.int32, (PROWS, BLK), 0)
        lane_ids = lax.broadcasted_iota(jnp.int32, (PROWS, BLK), 1)
        for j in range(PROWS):
            for b in range(nb):
                placed = jnp.where((row_ids == j) & (lane_ids == b), src_s[slab + j, b], placed)
        ids_out[PROWS : 2 * PROWS, 0:BLK] = placed
        if nb > 1:
            ids_out[PROWS : 2 * PROWS, BLK:] = jnp.zeros((PROWS, cells - BLK), jnp.int32)
        for copy in ring_copies:
            copy.start()

    for copies in lon_halos:
        for sends, _, copy in copies:
            gated(sends, copy.start)

    @pl.when(jnp.logical_not(polar))
    def _():
        for copy in centre:
            copy.wait()
        if middle:
            turn(middle)

    for sends, _, copy in lat_halos:
        gated(sends, copy.start)

    def tile(group, b, edge, chosen):
        row = pl.multiple_of(group * SUB, SUB)
        at = lanes(b)
        weights = weights_of(frac[pl.ds(row, SUB), at])
        anchors = off[pl.ds(row, SUB), at]
        results = {g: [] for g in chosen}
        for j in range(SUB):
            block_id = src_s[row + j, b]
            source_row = lax.div(block_id, NBLK) - first_row + HL
            source_row = jnp.clip(source_row, 0, rows + 2 * HL - 1)
            place = lax.rem(lax.rem(block_id, NBLK) - first_block + 1 + NBLK, NBLK)
            near = jnp.clip(place - 1, 0, nb - 1)
            far = jnp.minimum(place, 1)
            spot = jnp.full((SUB, BLK), place, jnp.int32)
            inside = (spot >= 1) & (spot <= nb)
            anchor = wide(anchors[j : j + 1])
            factors = [wide(w[j : j + 1]) for w in weights]
            for g in chosen:
                values = mid[source_row, near, pl.ds(g * SUB, SUB), :]
                if edge:
                    values = jnp.where(inside, values, sides[g][far, source_row])
                results[g].append(cubic_limited(values, anchor, factors))
        for g in chosen:
            out[g * SUB : (g + 1) * SUB, pl.ds(row, SUB), at] = jnp.swapaxes(
                jnp.stack(results[g]), 0, 1
            )

    tiles = rows // SUB

    def sweep(blocks, edge, chosen):
        count = len(blocks)
        if not count:
            return
        start, stride = blocks[0], (blocks[1] - blocks[0] if count > 1 else 1)

        @pl.loop(0, tiles * count)
        def _(step):
            group = lax.div(step, count)
            at_pole = ((lat == 0) & (group == 0)) | ((lat == n_lat - 1) & (group == tiles - 1))

            @pl.when(jnp.logical_not(at_pole))
            def _():
                tile(group, start + stride * lax.rem(step, count), edge, chosen)

    for _, receives, copy in lat_halos:
        gated(receives, copy.wait_recv)
    sweep(middle, False, range(groups))

    @pl.when(polar)
    def _():
        for copy in tables:
            copy.wait()
        ids[lon] = ids_out[...]
        fracs[lon] = frac[slab_at]
        ring[:, own] = mid[pl.ds(HL + slab, PROWS), :, pl.ds(group_of(lon), SUB), :]
        for copy in ring_copies:
            copy.wait_recv()
        fetch = pltpu.make_async_copy(
            ids.at[:, pl.ds(PROWS, PROWS), pl.ds(0, BLK)], ids_s, loc_sem.at[9]
        )
        fetch.start()
        fetch.wait()
        row_base = lax.div(lon, groups) * work_rows
        slab_global = first_row + slab
        pole = jnp.where(lat == 0, 0, 1)

        @pl.loop(0, work_rows)
        def _(j):
            jw = row_base + j
            band = []
            for b in range(NBLK):
                q, bb = b // nb, b % nb
                block_id = ids_s[q, jw, bb]
                source_row = jnp.clip(lax.div(block_id, NBLK) - slab_global, 0, PROWS - 1)
                values = ring[source_row, lax.rem(block_id, NBLK)]
                at = pl.ds(bb * BLK, BLK)
                weights = weights_of(row_of(fracs[q, :, at], jw))
                anchor = row_of(ids[q, 0:PROWS, at], jw)
                limited = cubic_limited(values, anchor, weights)
                lim[j, b] = limited
                band.append((limited, None))
            waves = fourier(band, -1)
            for k in range(HALF):
                re, im = waves[k]
                cosine, sine = wide(twd[0, k : k + 1, :]), wide(twd[1, k : k + 1, :])
                at = pl.ds(pl.multiple_of(k * tall + j * SUB, SUB), SUB)
                if im is None:
                    spec[at, 0:BLK] = re * cosine
                    spec[at, BLK : 2 * BLK] = -re * sine
                else:
                    spec[at, 0:BLK] = re * cosine + im * sine
                    spec[at, BLK : 2 * BLK] = im * cosine - re * sine

        def transform():
            spec[...] = jnp.dot(
                spec[...], mat[...], precision=lax.Precision.HIGHEST,
                preferred_element_type=jnp.float32,
            )

        transform()

        @pl.loop(0, work_rows)
        def _(j):
            kappa = cut_s[pole, row_base + j].astype(jnp.float32)
            for k in range(HALF):
                wave = k + NBLK * lax.broadcasted_iota(jnp.int32, (SUB, BLK), 1)
                wave = jnp.minimum(wave, NLON - wave)
                kept = (wave >= 1) & (wave < NLON // 2)
                damping = 1.0 - kappa / jnp.maximum(wave, 1).astype(jnp.float32)
                damping = jnp.where(kept, jnp.maximum(damping, 0.0), 0.0) * (1.0 / NLON)
                at = pl.ds(pl.multiple_of(k * tall + j * SUB, SUB), SUB)
                spec[at, 0:BLK] = spec[at, 0:BLK] * damping
                spec[at, BLK : 2 * BLK] = -spec[at, BLK : 2 * BLK] * damping

        transform()

        @pl.loop(0, work_rows)
        def _(j):
            waves = []
            for k in range(HALF):
                at = pl.ds(pl.multiple_of(k * tall + j * SUB, SUB), SUB)
                re, im = spec[at, 0:BLK], spec[at, BLK : 2 * BLK]
                cosine, sine = wide(twd[0, k : k + 1, :]), wide(twd[1, k : k + 1, :])
                real = re * cosine + im * sine
                waves.append((real, None if k in (0, HALF - 1) else re * sine - im * cosine))
            for k in range(HALF, NBLK):
                re, im = waves[NBLK - k]
                waves.append((re, -im))
            removed = fourier(waves, 1)
            for b in range(NBLK):
                done[j, b] = lim[j, b] - removed[b][0]

        for copy in back_copies:
            copy.start()
        back[pl.ds(row_base, work_rows), :, pl.ds(group_of(lon), SUB), :] = done[:, own]

    for g, copies in enumerate(lon_halos):
        for _, receives, copy in copies:
            gated(receives, copy.wait_recv)
        sweep(edges, True, [g])

    @pl.when(polar)
    def _():
        for copy in back_copies:
            copy.wait_recv()

        @pl.loop(0, groups)
        def _(g):
            ch = pl.multiple_of(g * SUB, SUB)
            for b in range(nb):
                at = slice(b * BLK, (b + 1) * BLK)
                out[pl.ds(ch, SUB), slab_at, at] = jnp.swapaxes(back[:, b, pl.ds(ch, SUB), :], 0, 1)

        for copy in ring_copies + back_copies:
            copy.wait_send()

    for sends, _, copy in lat_halos + sum(lon_halos, []):
        gated(sends, copy.wait_send)


def body(n_lat, n_lon, tracer, source, offset, fraction, cutoffs):
    channels, rows, cells = tracer.shape
    shares = n_lon // (channels // SUB)
    work_rows = PROWS // shares
    matrix, twiddle = dft_tables()
    dma = pltpu.SemaphoreType.DMA
    vmem = pl.BlockSpec(memory_space=pltpu.VMEM)
    return pl.pallas_call(
        functools.partial(kernel, n_lat, n_lon),
        out_shape=jax.ShapeDtypeStruct(tracer.shape, jnp.float32),
        in_specs=[pl.BlockSpec(memory_space=pl.ANY)] * 7,
        out_specs=vmem,
        scratch_shapes=[
            pltpu.SMEM(source.shape, jnp.int32),
            pltpu.SMEM(cutoffs.shape, jnp.int32),
            pltpu.VMEM(tracer.shape, jnp.float32),
            pltpu.VMEM(offset.shape, jnp.int32),
            pltpu.VMEM(fraction.shape, jnp.float32),
            pltpu.VMEM(matrix.shape, jnp.float32),
            pltpu.VMEM(twiddle.shape, jnp.float32),
            pltpu.VMEM((rows + 2 * HL, cells // BLK, channels, BLK), jnp.float32),
        ] + [pltpu.VMEM((2, rows + 2 * HL, SUB, BLK), jnp.float32)] * 4 + [
            pltpu.VMEM((PROWS, NBLK, SUB, BLK), jnp.float32),
            pltpu.VMEM((n_lon, 2 * PROWS, cells), jnp.int32),
            pltpu.VMEM((2 * PROWS, cells), jnp.int32),
            pltpu.VMEM((n_lon, PROWS, cells), jnp.float32),
            pltpu.SMEM((n_lon, PROWS, BLK), jnp.int32),
            pltpu.VMEM((work_rows, NBLK, SUB, BLK), jnp.float32),
            pltpu.VMEM((HALF * work_rows * SUB, 2 * BLK), jnp.float32),
            pltpu.VMEM((work_rows, NBLK, SUB, BLK), jnp.float32),
            pltpu.VMEM((PROWS, cells // BLK, channels, BLK), jnp.float32),
            dma((26,)), dma((26,)),
        ] + [dma((n_lon - 1,))] * 8 + [dma((10,))],
        compiler_params=pltpu.CompilerParams(
            collective_id=0, has_side_effects=True, vmem_limit_bytes=40 * 2**20
        ),
        cost_estimate=pl.CostEstimate(flops=10**9, bytes_accessed=5 * 10**6, transcendentals=0),
    )(source, cutoffs, tracer, offset, fraction, jnp.asarray(matrix), jnp.asarray(twiddle))


def solution(mesh):
    placed = (P(None, "lat", "lon"), P("lat", "lon"), P("lat", "lon"), P("lat", "lon"), P())
    step = functools.partial(body, mesh.shape["lat"], mesh.shape["lon"])
    return jax.shard_map(
        step, mesh=mesh, in_specs=placed, out_specs=P(None, "lat", "lon"), check_vma=False
    )
```

```python
import functools
import math

import jax
import jax.numpy as jnp
import numpy as np
from jax import lax
from jax.experimental import pallas as pl
from jax.experimental.pallas import tpu as pltpu
from jax.sharding import PartitionSpec as P

NLON = 2048
BLK = 128
HL = 2
PROWS = 8
NBLK = NLON // BLK
SUB = 8
HALF = NBLK // 2 + 1
MESH = pl.DeviceIdType.MESH


def dft_tables():
    lanes = np.arange(BLK)
    angles = 2.0 * math.pi * (np.outer(lanes, lanes) % BLK) / BLK
    cosines, sines = np.cos(angles), np.sin(angles)
    matrix = np.block([[cosines, -sines], [sines, cosines]])
    turns = 2.0 * math.pi * np.outer(np.arange(NBLK), lanes) / NLON
    twiddle = np.stack([np.cos(turns), np.sin(turns)])
    return matrix.astype(np.float32), twiddle.astype(np.float32)


def add(left, right):
    if left is None:
        return right
    return left if right is None else left + right


def sub(left, right):
    if right is None:
        return left
    return -right if left is None else left - right


def scaled(value, factor):
    return None if value is None or factor == 0.0 else value * factor


def turned(value, cosine, sine):
    re, im = value
    cosine, sine = (0.0 if abs(v) < 1e-12 else v for v in (cosine, sine))
    if sine == 0.0 and cosine == 1.0:
        return value
    if cosine == 0.0 and abs(sine) == 1.0:
        if sine > 0:
            return (None if im is None else -im), re
        return im, (None if re is None else -re)
    return sub(scaled(re, cosine), scaled(im, sine)), add(scaled(re, sine), scaled(im, cosine))


def fourier(values, sign):
    count = len(values)
    if count == 1:
        return values
    even, odd = fourier(values[::2], sign), fourier(values[1::2], sign)
    low, high = [], []
    for k in range(count // 2):
        angle = sign * 2.0 * math.pi * k / count
        re, im = turned(odd[k], math.cos(angle), math.sin(angle))
        low.append((add(even[k][0], re), add(even[k][1], im)))
        high.append((sub(even[k][0], re), sub(even[k][1], im)))
    return low + high


def weights_of(t):
    return (
        -t * (t - 1.0) * (t - 2.0) / 6.0,
        (t + 1.0) * (t - 1.0) * (t - 2.0) / 2.0,
        -(t + 1.0) * t * (t - 2.0) / 2.0,
        (t + 1.0) * t * (t - 1.0) / 6.0,
    )


def wide(row):
    return jnp.broadcast_to(row, (SUB, BLK))


def lanes_at(values, index):
    return jnp.take_along_axis(values, index, axis=1, mode="promise_in_bounds")


def row_of(values, row):
    index = jnp.full((SUB, BLK), row, jnp.int32)
    return jnp.take_along_axis(values, index, axis=0, mode="promise_in_bounds")


def cubic_limited(values, anchor, weights):
    before = lanes_at(values, anchor - 1)
    here = lanes_at(values, anchor)
    after = lanes_at(values, anchor + 1)
    beyond = lanes_at(values, anchor + 2)
    mixed = weights[0] * before + weights[1] * here + weights[2] * after + weights[3] * beyond
    return jnp.minimum(jnp.maximum(mixed, jnp.minimum(here, after)), jnp.maximum(here, after))


def lanes(block):
    return pl.ds(pl.multiple_of(block * BLK, BLK), BLK)


def kernel(
    n_lat, n_lon, src_h, cut_h, trc_h, off_h, frac_h, mat_h, twd_h, out,
    src_s, cut_s, trc, off, frac, mat, twd,
    mid, side_0, side_1, side_2, side_3, ring, ids, ids_out, fracs, ids_s, lim, spec, done, back,
    halo_send, halo_recv, pol_send, pol_recv, idx_send, idx_recv, frc_send, frc_recv,
    ret_send, ret_recv, loc_sem,
):
    sides = (side_0, side_1, side_2, side_3)
    channels, rows, cells = trc.shape
    nb = cells // BLK
    groups = channels // SUB
    shares = n_lon // groups
    work_rows = PROWS // shares
    tall = work_rows * SUB
    lat, lon = lax.axis_index("lat"), lax.axis_index("lon")
    first_row = lat * rows
    first_block = lon * nb
    right, left = lax.rem(lon + 1, n_lon), lax.rem(lon + n_lon - 1, n_lon)
    down, up = lax.rem(lat + 1, n_lat), lax.rem(lat + n_lat - 1, n_lat)
    polar = (lat == 0) | (lat == n_lat - 1)
    slab = jnp.where(lat == 0, 0, rows - PROWS)
    worker = (lat == 2) | (lat == n_lat - 3)
    northern = lat < n_lat // 2
    mate = jnp.where(northern, 2 - lat, 2 * n_lat - 4 - lat)
    pole = jnp.where(northern, 0, 1)
    peers = [lax.rem(lon + d, n_lon) for d in range(n_lon)]

    edges = sorted({0, nb - 1})
    middle = list(range(1, nb - 1))

    def local(src, dst, sem):
        return pltpu.make_async_copy(src, dst, loc_sem.at[sem])

    def block_span(first_block_in, count):
        return pl.ds(first_block_in * BLK, count * BLK)

    loads = [
        local(trc_h.at[:, :, block_span(b, 1)], trc.at[:, :, block_span(b, 1)], n)
        for n, b in enumerate(edges)
    ]
    small = [local(off_h, off, 2), local(frac_h, frac, 3), local(src_h, src_s, 4)]
    tables = [local(cut_h, cut_s, 5), local(mat_h, mat, 6), local(twd_h, twd, 7)]
    for copy in loads:
        copy.start()
    centre = []
    if middle:
        span = block_span(1, len(middle))
        centre = [local(trc_h.at[:, :, span], trc.at[:, :, span], 8)]
    for copy in small + centre:
        copy.start()

    @pl.when(worker)
    def _():
        for copy in tables:
            copy.start()

    barrier = pltpu.get_barrier_semaphore()
    for device in ((lat, left), (lat, right), (up, lon), (down, lon)):
        pl.semaphore_signal(barrier, inc=1, device_id=device, device_id_type=MESH)

    @pl.when(polar | worker)
    def _():
        for peer in peers:
            pl.semaphore_signal(barrier, inc=1, device_id=(mate, peer), device_id_type=MESH)

    def turn(blocks):
        @pl.loop(0, groups * (rows // SUB))
        def _(step):
            ch = pl.multiple_of(lax.rem(step, groups) * SUB, SUB)
            row = pl.multiple_of(lax.div(step, groups) * SUB, SUB)
            for b in blocks:
                tile = trc[pl.ds(ch, SUB), pl.ds(row, SUB), b * BLK : (b + 1) * BLK]
                mid[pl.ds(HL + row, SUB), b, pl.ds(ch, SUB), :] = jnp.swapaxes(tile, 0, 1)

    for copy in loads:
        copy.wait()
    turn(edges)

    pl.semaphore_wait(barrier, jnp.where(polar | worker, 4 + n_lon, 4))

    def group_of(place):
        return pl.multiple_of(lax.rem(place, groups) * SUB, SUB)

    def span_of(place):
        return pl.ds(place * nb, nb)

    def remote(src, dst, send, recv, device):
        return pltpu.make_async_remote_copy(
            src_ref=src, dst_ref=dst, send_sem=send, recv_sem=recv,
            device_id=device, device_id_type=MESH,
        )

    slab_at = pl.ds(pl.multiple_of(slab, SUB), PROWS)
    own = span_of(lon)
    ring_copies, back_copies = [], []
    for d, peer in enumerate(peers):
        ring_copies += [
            remote(ids_out, ids.at[lon], idx_send.at[d], idx_recv.at[d], (mate, peer)),
            remote(frac.at[slab_at], fracs.at[lon], frc_send.at[d], frc_recv.at[d], (mate, peer)),
            remote(
                mid.at[pl.ds(HL + slab, PROWS), :, pl.ds(group_of(peer), SUB), :],
                ring.at[:, own],
                pol_send.at[d], pol_recv.at[d], (mate, peer),
            ),
        ]
        back_copies.append(
            remote(
                done.at[:, span_of(peer)],
                back.at[
                    pl.ds(lax.div(lon, groups) * work_rows, work_rows), :, pl.ds(group_of(lon), SUB), :
                ],
                ret_send.at[d], ret_recv.at[d], (mate, peer),
            )
        )

    first, last = 0, nb - 1
    top, bottom = pl.ds(HL, HL), pl.ds(rows, HL)
    over, under = pl.ds(0, HL), pl.ds(HL + rows, HL)
    inner = pl.ds(2 * HL, rows - 2 * HL)
    some = pl.ds(jnp.where(lat == 0, PROWS, 2 * HL), rows - PROWS)
    has_up, has_down = lat > 0, lat < n_lat - 1
    counter = iter(range(100))

    def halo(src, dst, device):
        n = next(counter)
        return remote(src, dst, halo_send.at[n], halo_recv.at[n], device)

    lat_halos = [
        (has_down, has_up, halo(mid.at[bottom], mid.at[over], (down, lon))),
        (has_up, has_down, halo(mid.at[top], mid.at[under], (up, lon))),
    ]
    lon_halos, rims, passed = [], [], []
    for g in range(groups):
        chans, side = pl.ds(g * SUB, SUB), sides[g]
        copies = []
        for to, block, half in ((right, last, 0), (left, first, 1)):
            n = next(counter)
            for span, when in ((inner, jnp.logical_not(polar)), (some, polar)):
                copies.append((when, when, remote(
                    mid.at[span, block, chans], side.at[half, span],
                    halo_send.at[n], halo_recv.at[n], (lat, to),
                )))
            for span, when in ((top, has_up), (bottom, has_down)):
                rims.append((when, when, halo(
                    mid.at[span, block, chans], side.at[half, span], (lat, to))))
            forward = [
                (has_down, has_up, halo(side.at[half, bottom], side.at[half, over], (down, lon))),
                (has_up, has_down, halo(side.at[half, top], side.at[half, under], (up, lon))),
            ]
            passed += forward
            copies += forward
        lon_halos.append(copies)

    def gated(condition, action):
        @pl.when(condition)
        def _():
            action()

    for copy in small:
        copy.wait()

    @pl.when(polar)
    def _():
        for copy in centre:
            copy.wait()
        if middle:
            turn(middle)
        ids_out[0:PROWS] = off[slab_at]
        placed = jnp.zeros((PROWS, BLK), jnp.int32)
        row_ids = lax.broadcasted_iota(jnp.int32, (PROWS, BLK), 0)
        lane_ids = lax.broadcasted_iota(jnp.int32, (PROWS, BLK), 1)
        for j in range(PROWS):
            for b in range(nb):
                placed = jnp.where((row_ids == j) & (lane_ids == b), src_s[b, slab + j], placed)
        ids_out[PROWS : 2 * PROWS, 0:BLK] = placed
        if nb > 1:
            ids_out[PROWS : 2 * PROWS, BLK:] = jnp.zeros((PROWS, cells - BLK), jnp.int32)
        for copy in ring_copies:
            copy.start()

    for sends, _, copy in rims:
        gated(sends, copy.start)
    for copies in lon_halos:
        for sends, _, copy in copies:
            if all(copy is not other for _, _, other in passed):
                gated(sends, copy.start)

    @pl.when(jnp.logical_not(polar))
    def _():
        for copy in centre:
            copy.wait()
        if middle:
            turn(middle)

    for sends, _, copy in lat_halos:
        gated(sends, copy.start)

    def tile(group, b, edge, chosen):
        row = pl.multiple_of(group * SUB, SUB)
        at = lanes(b)
        weights = weights_of(frac[pl.ds(row, SUB), at])
        anchors = off[pl.ds(row, SUB), at]
        results = {g: [] for g in chosen}
        for j in range(SUB):
            block_id = src_s[b, row + j]
            source_row = lax.div(block_id, NBLK) - first_row + HL
            source_row = jnp.clip(source_row, 0, rows + 2 * HL - 1)
            place = lax.rem(lax.rem(block_id, NBLK) - first_block + 1 + NBLK, NBLK)
            near = jnp.clip(place - 1, 0, nb - 1)
            far = jnp.minimum(place, 1)
            spot = jnp.full((SUB, BLK), place, jnp.int32)
            inside = (spot >= 1) & (spot <= nb)
            anchor = wide(anchors[j : j + 1])
            factors = [wide(w[j : j + 1]) for w in weights]
            for g in chosen:
                values = mid[source_row, near, pl.ds(g * SUB, SUB), :]
                if edge:
                    values = jnp.where(inside, values, sides[g][far, source_row])
                results[g].append(cubic_limited(values, anchor, factors))
        for g in chosen:
            out[g * SUB : (g + 1) * SUB, pl.ds(row, SUB), at] = jnp.swapaxes(
                jnp.stack(results[g]), 0, 1
            )

    tiles = rows // SUB

    def sweep(blocks, edge, chosen):
        count = len(blocks)
        if not count:
            return
        start, stride = blocks[0], (blocks[1] - blocks[0] if count > 1 else 1)

        @pl.loop(0, tiles * count)
        def _(step):
            group = lax.div(step, count)
            at_pole = ((lat == 0) & (group == 0)) | ((lat == n_lat - 1) & (group == tiles - 1))

            @pl.when(jnp.logical_not(at_pole))
            def _():
                tile(group, start + stride * lax.rem(step, count), edge, chosen)

    for _, receives, copy in rims:
        gated(receives, copy.wait_recv)
    for sends, _, copy in passed:
        gated(sends, copy.start)
    for _, receives, copy in lat_halos:
        gated(receives, copy.wait_recv)
    sweep(middle, False, range(groups))

    @pl.when(worker)
    def _():
        for copy in tables:
            copy.wait()
        for copy in ring_copies:
            copy.wait_recv()
        fetch = pltpu.make_async_copy(
            ids.at[:, pl.ds(PROWS, PROWS), pl.ds(0, BLK)], ids_s, loc_sem.at[9]
        )
        fetch.start()
        fetch.wait()
        row_base = lax.div(lon, groups) * work_rows
        slab_global = jnp.where(northern, 0, n_lat * rows - PROWS)

        @pl.loop(0, work_rows)
        def _(j):
            jw = row_base + j
            band = []
            for b in range(NBLK):
                q, bb = b // nb, b % nb
                block_id = ids_s[q, jw, bb]
                source_row = jnp.clip(lax.div(block_id, NBLK) - slab_global, 0, PROWS - 1)
                values = ring[source_row, lax.rem(block_id, NBLK)]
                at = pl.ds(bb * BLK, BLK)
                weights = weights_of(row_of(fracs[q, :, at], jw))
                anchor = row_of(ids[q, 0:PROWS, at], jw)
                limited = cubic_limited(values, anchor, weights)
                lim[j, b] = limited
                band.append((limited, None))
            waves = fourier(band, -1)
            for k in range(HALF):
                re, im = waves[k]
                cosine, sine = wide(twd[0, k : k + 1, :]), wide(twd[1, k : k + 1, :])
                at = pl.ds(pl.multiple_of(k * tall + j * SUB, SUB), SUB)
                if im is None:
                    spec[at, 0:BLK] = re * cosine
                    spec[at, BLK : 2 * BLK] = -re * sine
                else:
                    spec[at, 0:BLK] = re * cosine + im * sine
                    spec[at, BLK : 2 * BLK] = im * cosine - re * sine

        def transform():
            spec[...] = jnp.dot(
                spec[...], mat[...], precision=lax.Precision.HIGHEST,
                preferred_element_type=jnp.float32,
            )

        transform()

        @pl.loop(0, work_rows)
        def _(j):
            kappa = cut_s[pole, row_base + j].astype(jnp.float32)
            for k in range(HALF):
                wave = k + NBLK * lax.broadcasted_iota(jnp.int32, (SUB, BLK), 1)
                wave = jnp.minimum(wave, NLON - wave)
                kept = (wave >= 1) & (wave < NLON // 2)
                damping = 1.0 - kappa / jnp.maximum(wave, 1).astype(jnp.float32)
                damping = jnp.where(kept, jnp.maximum(damping, 0.0), 0.0) * (1.0 / NLON)
                at = pl.ds(pl.multiple_of(k * tall + j * SUB, SUB), SUB)
                spec[at, 0:BLK] = spec[at, 0:BLK] * damping
                spec[at, BLK : 2 * BLK] = -spec[at, BLK : 2 * BLK] * damping

        transform()

        @pl.loop(0, work_rows)
        def _(j):
            waves = []
            for k in range(HALF):
                at = pl.ds(pl.multiple_of(k * tall + j * SUB, SUB), SUB)
                re, im = spec[at, 0:BLK], spec[at, BLK : 2 * BLK]
                cosine, sine = wide(twd[0, k : k + 1, :]), wide(twd[1, k : k + 1, :])
                real = re * cosine + im * sine
                waves.append((real, None if k in (0, HALF - 1) else re * sine - im * cosine))
            for k in range(HALF, NBLK):
                re, im = waves[NBLK - k]
                waves.append((re, -im))
            removed = fourier(waves, 1)
            for b in range(NBLK):
                done[j, b] = lim[j, b] - removed[b][0]

        for copy in back_copies:
            copy.start()

    for g, copies in enumerate(lon_halos):
        for _, receives, copy in copies:
            gated(receives, copy.wait_recv)
        sweep(edges, True, [g])

    @pl.when(polar)
    def _():
        for copy in back_copies:
            copy.wait_recv()

        @pl.loop(0, groups)
        def _(g):
            ch = pl.multiple_of(g * SUB, SUB)
            for b in range(nb):
                at = slice(b * BLK, (b + 1) * BLK)
                out[pl.ds(ch, SUB), slab_at, at] = jnp.swapaxes(back[:, b, pl.ds(ch, SUB), :], 0, 1)

        for copy in ring_copies:
            copy.wait_send()

    @pl.when(worker)
    def _():
        for copy in back_copies:
            copy.wait_send()

    for sends, _, copy in lat_halos + rims + sum(lon_halos, []):
        gated(sends, copy.wait_send)


def body(n_lat, n_lon, tracer, source, offset, fraction, cutoffs):
    channels, rows, cells = tracer.shape
    shares = n_lon // (channels // SUB)
    work_rows = PROWS // shares
    matrix, twiddle = dft_tables()
    dma = pltpu.SemaphoreType.DMA
    vmem = pl.BlockSpec(memory_space=pltpu.VMEM)
    return pl.pallas_call(
        functools.partial(kernel, n_lat, n_lon),
        out_shape=jax.ShapeDtypeStruct(tracer.shape, jnp.float32),
        in_specs=[pl.BlockSpec(memory_space=pltpu.HBM)] * 7,
        out_specs=vmem,
        scratch_shapes=[
            pltpu.SMEM(source.shape[::-1], jnp.int32),
            pltpu.SMEM(cutoffs.shape, jnp.int32),
            pltpu.VMEM(tracer.shape, jnp.float32),
            pltpu.VMEM(offset.shape, jnp.int32),
            pltpu.VMEM(fraction.shape, jnp.float32),
            pltpu.VMEM(matrix.shape, jnp.float32),
            pltpu.VMEM(twiddle.shape, jnp.float32),
            pltpu.VMEM((rows + 2 * HL, cells // BLK, channels, BLK), jnp.float32),
        ] + [pltpu.VMEM((2, rows + 2 * HL, SUB, BLK), jnp.float32)] * 4 + [
            pltpu.VMEM((PROWS, NBLK, SUB, BLK), jnp.float32),
            pltpu.VMEM((n_lon, 2 * PROWS, cells), jnp.int32),
            pltpu.VMEM((2 * PROWS, cells), jnp.int32),
            pltpu.VMEM((n_lon, PROWS, cells), jnp.float32),
            pltpu.SMEM((n_lon, PROWS, BLK), jnp.int32),
            pltpu.VMEM((work_rows, NBLK, SUB, BLK), jnp.float32),
            pltpu.VMEM((HALF * work_rows * SUB, 2 * BLK), jnp.float32),
            pltpu.VMEM((work_rows, NBLK, SUB, BLK), jnp.float32),
            pltpu.VMEM((PROWS, cells // BLK, channels, BLK), jnp.float32),
            dma((42,)), dma((42,)),
        ] + [dma((n_lon,))] * 8 + [dma((10,))],
        compiler_params=pltpu.CompilerParams(
            collective_id=0, has_side_effects=True, vmem_limit_bytes=64 * 2**20 - 2**16
        ),
        cost_estimate=pl.CostEstimate(flops=10**9, bytes_accessed=5 * 10**6, transcendentals=0),
    )(source.T, cutoffs, tracer, offset, fraction, jnp.asarray(matrix), jnp.asarray(twiddle))


def solution(mesh):
    placed = (P(None, "lat", "lon"), P("lat", "lon"), P("lat", "lon"), P("lat", "lon"), P())
    step = functools.partial(body, mesh.shape["lat"], mesh.shape["lon"])
    return jax.shard_map(
        step, mesh=mesh, in_specs=placed, out_specs=P(None, "lat", "lon"), check_vma=False
    )
```

```python
import functools
import math

import jax
import jax.numpy as jnp
import numpy as np
from jax import lax
from jax.experimental import pallas as pl
from jax.experimental.pallas import tpu as pltpu
from jax.sharding import PartitionSpec as P

NLON = 2048
BLK = 128
HL = 2
PROWS = 8
NBLK = NLON // BLK
SUB = 8
HALF = NBLK // 2 + 1
MESH = pl.DeviceIdType.MESH
VMEM_LIMIT = 64 * 2**20 - 2**16


def dft_tables():
    lanes = np.arange(BLK)
    angles = 2.0 * math.pi * (np.outer(lanes, lanes) % BLK) / BLK
    cosines, sines = np.cos(angles), np.sin(angles)
    matrix = np.block([[cosines, -sines], [sines, cosines]])
    turns = 2.0 * math.pi * np.outer(np.arange(NBLK), lanes) / NLON
    twiddle = np.stack([np.cos(turns), np.sin(turns)])
    return matrix.astype(np.float32), twiddle.astype(np.float32)


def add(left, right):
    if left is None:
        return right
    return left if right is None else left + right


def sub(left, right):
    if right is None:
        return left
    return -right if left is None else left - right


def scaled(value, factor):
    return None if value is None or factor == 0.0 else value * factor


def turned(value, cosine, sine):
    re, im = value
    cosine, sine = (0.0 if abs(v) < 1e-12 else v for v in (cosine, sine))
    if sine == 0.0 and cosine == 1.0:
        return value
    if cosine == 0.0 and abs(sine) == 1.0:
        if sine > 0:
            return (None if im is None else -im), re
        return im, (None if re is None else -re)
    return sub(scaled(re, cosine), scaled(im, sine)), add(scaled(re, sine), scaled(im, cosine))


def fourier(values, sign):
    count = len(values)
    if count == 1:
        return values
    even, odd = fourier(values[::2], sign), fourier(values[1::2], sign)
    low, high = [], []
    for k in range(count // 2):
        angle = sign * 2.0 * math.pi * k / count
        re, im = turned(odd[k], math.cos(angle), math.sin(angle))
        low.append((add(even[k][0], re), add(even[k][1], im)))
        high.append((sub(even[k][0], re), sub(even[k][1], im)))
    return low + high


def weights_of(t):
    return (
        -t * (t - 1.0) * (t - 2.0) / 6.0,
        (t + 1.0) * (t - 1.0) * (t - 2.0) / 2.0,
        -(t + 1.0) * t * (t - 2.0) / 2.0,
        (t + 1.0) * t * (t - 1.0) / 6.0,
    )


def halves(values):
    upper = values.astype(jnp.bfloat16)
    return upper, (values - upper.astype(jnp.float32)).astype(jnp.bfloat16)


def wide(row):
    return jnp.broadcast_to(row, (SUB, BLK))


def lanes_at(values, index):
    return jnp.take_along_axis(values, index, axis=1, mode="promise_in_bounds")


def row_of(values, row):
    index = jnp.full((SUB, BLK), row, jnp.int32)
    return jnp.take_along_axis(values, index, axis=0, mode="promise_in_bounds")


def cubic_limited(values, anchor, weights):
    before = lanes_at(values, anchor - 1)
    here = lanes_at(values, anchor)
    after = lanes_at(values, anchor + 1)
    beyond = lanes_at(values, anchor + 2)
    mixed = weights[0] * before + weights[1] * here + weights[2] * after + weights[3] * beyond
    return jnp.minimum(jnp.maximum(mixed, jnp.minimum(here, after)), jnp.maximum(here, after))


def lanes(block):
    return pl.ds(pl.multiple_of(block * BLK, BLK), BLK)


def kernel(
    n_lat, n_lon, src_h, cut_h, trc_h, off_h, frac_h, mat_h, twd_h, out,
    src_s, cut_s, trc, off, frac, mat, twd,
    mid, side_0, side_1, side_2, side_3, ring, ids, ids_out, fracs, ids_s, lim, spec, done, back,
    halo_send, halo_recv, pol_send, pol_recv, idx_send, idx_recv, frc_send, frc_recv,
    ret_send, ret_recv, loc_sem,
):
    sides = (side_0, side_1, side_2, side_3)
    channels, rows, cells = trc.shape
    nb = cells // BLK
    groups = channels // SUB
    shares = n_lon // groups
    work_rows = PROWS // shares
    tall = work_rows * SUB
    lat, lon = lax.axis_index("lat"), lax.axis_index("lon")
    first_row = lat * rows
    first_block = lon * nb
    right, left = lax.rem(lon + 1, n_lon), lax.rem(lon + n_lon - 1, n_lon)
    down, up = lax.rem(lat + 1, n_lat), lax.rem(lat + n_lat - 1, n_lat)
    polar = (lat == 0) | (lat == n_lat - 1)
    slab = jnp.where(lat == 0, 0, rows - PROWS)
    worker = (lat == 2) | (lat == n_lat - 3)
    northern = lat < n_lat // 2
    mate = jnp.where(northern, 2 - lat, 2 * n_lat - 4 - lat)
    pole = jnp.where(northern, 0, 1)
    peers = [lax.rem(lon + d, n_lon) for d in range(n_lon)]

    edges = sorted({0, nb - 1})
    middle = list(range(1, nb - 1))

    def local(src, dst, sem):
        return pltpu.make_async_copy(src, dst, loc_sem.at[sem])

    def block_span(first_block_in, count):
        return pl.ds(first_block_in * BLK, count * BLK)

    loads = [
        local(trc_h.at[:, :, block_span(b, 1)], trc.at[:, :, block_span(b, 1)], n)
        for n, b in enumerate(edges)
    ]
    small = [local(off_h, off, 2), local(frac_h, frac, 3), local(src_h, src_s, 4)]
    tables = [local(cut_h, cut_s, 5), local(mat_h, mat, 6), local(twd_h, twd, 7)]
    for copy in loads:
        copy.start()
    centre = []
    if middle:
        span = block_span(1, len(middle))
        centre = [local(trc_h.at[:, :, span], trc.at[:, :, span], 8)]
    for copy in small + centre:
        copy.start()

    @pl.when(worker)
    def _():
        for copy in tables:
            copy.start()

    barrier = pltpu.get_barrier_semaphore()
    for device in ((lat, left), (lat, right), (up, lon), (down, lon)):
        pl.semaphore_signal(barrier, inc=1, device_id=device, device_id_type=MESH)

    @pl.when(polar | worker)
    def _():
        for peer in peers:
            pl.semaphore_signal(barrier, inc=1, device_id=(mate, peer), device_id_type=MESH)

    def turn(blocks, row_groups, skip_pole):
        @pl.loop(0, groups * len(row_groups))
        def _(step):
            ch = pl.multiple_of(lax.rem(step, groups) * SUB, SUB)
            index = lax.div(step, groups)
            row = pl.multiple_of(index * SUB if len(row_groups) > 1 else row_groups[0], SUB)

            def move():
                for b in blocks:
                    tile = trc[pl.ds(ch, SUB), pl.ds(row, SUB), b * BLK : (b + 1) * BLK]
                    mid[pl.ds(HL + row, SUB), b, pl.ds(ch, SUB), :] = jnp.swapaxes(tile, 0, 1)

            if skip_pole:
                pl.when(jnp.logical_not(polar & (row == slab)))(move)
            else:
                move()

    every = range(rows // SUB)
    for copy in loads:
        copy.wait()

    @pl.when(polar)
    def _():
        for copy in centre:
            copy.wait()
        turn(edges + middle, [slab], False)

    @pl.when(jnp.logical_not(polar))
    def _():
        turn(edges, every, False)

    pl.semaphore_wait(barrier, jnp.where(polar | worker, 4 + n_lon, 4))

    def group_of(place):
        return pl.multiple_of(lax.rem(place, groups) * SUB, SUB)

    def span_of(place):
        return pl.ds(place * nb, nb)

    def remote(src, dst, send, recv, device):
        return pltpu.make_async_remote_copy(
            src_ref=src, dst_ref=dst, send_sem=send, recv_sem=recv,
            device_id=device, device_id_type=MESH,
        )

    slab_at = pl.ds(pl.multiple_of(slab, SUB), PROWS)
    own = span_of(lon)
    ring_copies, back_copies = [], []
    for d, peer in enumerate(peers):
        ring_copies += [
            remote(ids_out, ids.at[lon], idx_send.at[d], idx_recv.at[d], (mate, peer)),
            remote(frac.at[slab_at], fracs.at[lon], frc_send.at[d], frc_recv.at[d], (mate, peer)),
            remote(
                mid.at[pl.ds(HL + slab, PROWS), :, pl.ds(group_of(peer), SUB), :],
                ring.at[:, own],
                pol_send.at[d], pol_recv.at[d], (mate, peer),
            ),
        ]
        back_copies.append(
            remote(
                done.at[:, span_of(peer)],
                back.at[
                    pl.ds(lax.div(lon, groups) * work_rows, work_rows), :, pl.ds(group_of(lon), SUB), :
                ],
                ret_send.at[d], ret_recv.at[d], (mate, peer),
            )
        )

    first, last = 0, nb - 1
    top, bottom = pl.ds(HL, HL), pl.ds(rows, HL)
    over, under = pl.ds(0, HL), pl.ds(HL + rows, HL)
    inner = pl.ds(2 * HL, rows - 2 * HL)
    some = pl.ds(jnp.where(lat == 0, PROWS, 2 * HL), rows - PROWS)
    has_up, has_down = lat > 0, lat < n_lat - 1
    counter = iter(range(100))

    def halo(src, dst, device):
        n = next(counter)
        return remote(src, dst, halo_send.at[n], halo_recv.at[n], device)

    lat_halos = [
        (has_down, has_up, halo(mid.at[bottom], mid.at[over], (down, lon))),
        (has_up, has_down, halo(mid.at[top], mid.at[under], (up, lon))),
    ]
    lon_halos, rims, passed = [], [], []
    for g in range(groups):
        chans, side = pl.ds(g * SUB, SUB), sides[g]
        copies = []
        for to, block, half in ((right, last, 0), (left, first, 1)):
            n = next(counter)
            for span, when in ((inner, jnp.logical_not(polar)), (some, polar)):
                copies.append((when, when, remote(
                    mid.at[span, block, chans], side.at[half, span],
                    halo_send.at[n], halo_recv.at[n], (lat, to),
                )))
            for span, when in ((top, has_up), (bottom, has_down)):
                rims.append((when, when, halo(
                    mid.at[span, block, chans], side.at[half, span], (lat, to))))
            forward = [
                (has_down, has_up, halo(side.at[half, bottom], side.at[half, over], (down, lon))),
                (has_up, has_down, halo(side.at[half, top], side.at[half, under], (up, lon))),
            ]
            passed += forward
            copies += forward
        lon_halos.append(copies)

    def gated(condition, action):
        @pl.when(condition)
        def _():
            action()

    for copy in small:
        copy.wait()

    @pl.when(polar)
    def _():
        ids_out[0:PROWS] = off[slab_at]
        placed = jnp.zeros((PROWS, BLK), jnp.int32)
        row_ids = lax.broadcasted_iota(jnp.int32, (PROWS, BLK), 0)
        lane_ids = lax.broadcasted_iota(jnp.int32, (PROWS, BLK), 1)
        for j in range(PROWS):
            for b in range(nb):
                placed = jnp.where((row_ids == j) & (lane_ids == b), src_s[b, slab + j], placed)
        ids_out[PROWS : 2 * PROWS, 0:BLK] = placed
        if nb > 1:
            ids_out[PROWS : 2 * PROWS, BLK:] = jnp.zeros((PROWS, cells - BLK), jnp.int32)
        for copy in ring_copies:
            copy.start()
        turn(edges + middle, every, True)

    def send_group(g):
        for sends, _, copy in lon_halos[g]:
            if all(copy is not other for _, _, other in passed):
                gated(sends, copy.start)

    for sends, _, copy in rims:
        gated(sends, copy.start)
    ahead = 2
    for g in range(ahead):
        send_group(g)

    @pl.when(jnp.logical_not(polar))
    def _():
        for copy in centre:
            copy.wait()
        if middle:
            turn(middle, every, False)

    for sends, _, copy in lat_halos:
        gated(sends, copy.start)

    def tile(group, b, edge, chosen):
        row = pl.multiple_of(group * SUB, SUB)
        at = lanes(b)
        weights = weights_of(frac[pl.ds(row, SUB), at])
        anchors = off[pl.ds(row, SUB), at]
        results = {g: [] for g in chosen}
        for j in range(SUB):
            block_id = src_s[b, row + j]
            source_row = lax.div(block_id, NBLK) - first_row + HL
            source_row = jnp.clip(source_row, 0, rows + 2 * HL - 1)
            place = lax.rem(lax.rem(block_id, NBLK) - first_block + 1 + NBLK, NBLK)
            near = jnp.clip(place - 1, 0, nb - 1)
            far = jnp.minimum(place, 1)
            spot = jnp.full((SUB, BLK), place, jnp.int32)
            inside = (spot >= 1) & (spot <= nb)
            anchor = wide(anchors[j : j + 1])
            factors = [wide(w[j : j + 1]) for w in weights]
            for g in chosen:
                values = mid[source_row, near, pl.ds(g * SUB, SUB), :]
                if edge:
                    values = jnp.where(inside, values, sides[g][far, source_row])
                results[g].append(cubic_limited(values, anchor, factors))
        for g in chosen:
            out[g * SUB : (g + 1) * SUB, pl.ds(row, SUB), at] = jnp.swapaxes(
                jnp.stack(results[g]), 0, 1
            )

    tiles = rows // SUB

    def sweep(blocks, edge, chosen):
        count = len(blocks)
        if not count:
            return
        start, stride = blocks[0], (blocks[1] - blocks[0] if count > 1 else 1)

        @pl.loop(0, tiles * count)
        def _(step):
            group = lax.div(step, count)
            at_pole = ((lat == 0) & (group == 0)) | ((lat == n_lat - 1) & (group == tiles - 1))

            @pl.when(jnp.logical_not(at_pole))
            def _():
                tile(group, start + stride * lax.rem(step, count), edge, chosen)

    for _, receives, copy in rims:
        gated(receives, copy.wait_recv)
    for sends, _, copy in passed:
        gated(sends, copy.start)
    for _, receives, copy in lat_halos:
        gated(receives, copy.wait_recv)
    sweep(middle, False, range(groups))

    @pl.when(worker)
    def _():
        for copy in tables:
            copy.wait()
        for copy in ring_copies:
            copy.wait_recv()
        fetch = pltpu.make_async_copy(
            ids.at[:, pl.ds(PROWS, PROWS), pl.ds(0, BLK)], ids_s, loc_sem.at[9]
        )
        fetch.start()
        fetch.wait()
        row_base = lax.div(lon, groups) * work_rows
        slab_global = jnp.where(northern, 0, n_lat * rows - PROWS)

        @pl.loop(0, work_rows)
        def _(j):
            jw = row_base + j
            band = []
            for b in range(NBLK):
                q, bb = b // nb, b % nb
                block_id = ids_s[q, jw, bb]
                source_row = jnp.clip(lax.div(block_id, NBLK) - slab_global, 0, PROWS - 1)
                values = ring[source_row, lax.rem(block_id, NBLK)]
                at = pl.ds(bb * BLK, BLK)
                weights = weights_of(row_of(fracs[q, :, at], jw))
                anchor = row_of(ids[q, 0:PROWS, at], jw)
                limited = cubic_limited(values, anchor, weights)
                lim[j, b] = limited
                band.append((limited, None))
            waves = fourier(band, -1)
            for k in range(HALF):
                re, im = waves[k]
                cosine, sine = wide(twd[0, k : k + 1, :]), wide(twd[1, k : k + 1, :])
                at = pl.ds(pl.multiple_of(k * tall + j * SUB, SUB), SUB)
                if im is None:
                    spec[at, 0:BLK] = re * cosine
                    spec[at, BLK : 2 * BLK] = -re * sine
                else:
                    spec[at, 0:BLK] = re * cosine + im * sine
                    spec[at, BLK : 2 * BLK] = im * cosine - re * sine

        def transform():
            upper, lower = halves(spec[...])
            mat_upper, mat_lower = halves(mat[...])
            product = functools.partial(jnp.dot, preferred_element_type=jnp.float32)
            spec[...] = product(upper, mat_upper) + (
                product(lower, mat_upper) + product(upper, mat_lower)
            )

        transform()

        @pl.loop(0, work_rows)
        def _(j):
            kappa = cut_s[pole, row_base + j].astype(jnp.float32)
            for k in range(HALF):
                wave = k + NBLK * lax.broadcasted_iota(jnp.int32, (SUB, BLK), 1)
                wave = jnp.minimum(wave, NLON - wave)
                kept = (wave >= 1) & (wave < NLON // 2)
                damping = 1.0 - kappa / jnp.maximum(wave, 1).astype(jnp.float32)
                damping = jnp.where(kept, jnp.maximum(damping, 0.0), 0.0) * (1.0 / NLON)
                at = pl.ds(pl.multiple_of(k * tall + j * SUB, SUB), SUB)
                spec[at, 0:BLK] = spec[at, 0:BLK] * damping
                spec[at, BLK : 2 * BLK] = -spec[at, BLK : 2 * BLK] * damping

        transform()

        @pl.loop(0, work_rows)
        def _(j):
            waves = []
            for k in range(HALF):
                at = pl.ds(pl.multiple_of(k * tall + j * SUB, SUB), SUB)
                re, im = spec[at, 0:BLK], spec[at, BLK : 2 * BLK]
                cosine, sine = wide(twd[0, k : k + 1, :]), wide(twd[1, k : k + 1, :])
                real = re * cosine + im * sine
                waves.append((real, None if k in (0, HALF - 1) else re * sine - im * cosine))
            for k in range(HALF, NBLK):
                re, im = waves[NBLK - k]
                waves.append((re, -im))
            removed = fourier(waves, 1)
            for b in range(NBLK):
                done[j, b] = lim[j, b] - removed[b][0]

        for copy in back_copies:
            copy.start()

    for g, copies in enumerate(lon_halos):
        for _, receives, copy in copies:
            gated(receives, copy.wait_recv)
        if g + ahead < groups:
            send_group(g + ahead)
        sweep(edges, True, [g])

    @pl.when(polar)
    def _():
        for copy in back_copies:
            copy.wait_recv()

        @pl.loop(0, groups)
        def _(g):
            ch = pl.multiple_of(g * SUB, SUB)
            for b in range(nb):
                at = slice(b * BLK, (b + 1) * BLK)
                out[pl.ds(ch, SUB), slab_at, at] = jnp.swapaxes(back[:, b, pl.ds(ch, SUB), :], 0, 1)

        for copy in ring_copies:
            copy.wait_send()

    @pl.when(worker)
    def _():
        for copy in back_copies:
            copy.wait_send()

    for sends, _, copy in lat_halos + rims + sum(lon_halos, []):
        gated(sends, copy.wait_send)


def write_out(values, out):
    out[...] = values[...]


def body(n_lat, n_lon, tracer, source, offset, fraction, cutoffs):
    channels, rows, cells = tracer.shape
    shares = n_lon // (channels // SUB)
    work_rows = PROWS // shares
    matrix, twiddle = dft_tables()
    dma = pltpu.SemaphoreType.DMA
    vmem = pl.BlockSpec(memory_space=pltpu.VMEM)
    result = pl.pallas_call(
        functools.partial(kernel, n_lat, n_lon),
        out_shape=jax.ShapeDtypeStruct(tracer.shape, jnp.float32),
        in_specs=[pl.BlockSpec(memory_space=pltpu.HBM)] * 7,
        out_specs=vmem,
        scratch_shapes=[
            pltpu.SMEM(source.shape[::-1], jnp.int32),
            pltpu.SMEM(cutoffs.shape, jnp.int32),
            pltpu.VMEM(tracer.shape, jnp.float32),
            pltpu.VMEM(offset.shape, jnp.int32),
            pltpu.VMEM(fraction.shape, jnp.float32),
            pltpu.VMEM(matrix.shape, jnp.float32),
            pltpu.VMEM(twiddle.shape, jnp.float32),
            pltpu.VMEM((rows + 2 * HL, cells // BLK, channels, BLK), jnp.float32),
        ] + [pltpu.VMEM((2, rows + 2 * HL, SUB, BLK), jnp.float32)] * 4 + [
            pltpu.VMEM((PROWS, NBLK, SUB, BLK), jnp.float32),
            pltpu.VMEM((n_lon, 2 * PROWS, cells), jnp.int32),
            pltpu.VMEM((2 * PROWS, cells), jnp.int32),
            pltpu.VMEM((n_lon, PROWS, cells), jnp.float32),
            pltpu.SMEM((n_lon, PROWS, BLK), jnp.int32),
            pltpu.VMEM((work_rows, NBLK, SUB, BLK), jnp.float32),
            pltpu.VMEM((HALF * work_rows * SUB, 2 * BLK), jnp.float32),
            pltpu.VMEM((work_rows, NBLK, SUB, BLK), jnp.float32),
            pltpu.VMEM((PROWS, cells // BLK, channels, BLK), jnp.float32),
            dma((42,)), dma((42,)),
        ] + [dma((n_lon,))] * 8 + [dma((10,))],
        compiler_params=pltpu.CompilerParams(
            collective_id=0, has_side_effects=True, vmem_limit_bytes=VMEM_LIMIT
        ),
        cost_estimate=pl.CostEstimate(flops=10**9, bytes_accessed=5 * 10**6, transcendentals=0),
    )(source.T, cutoffs, tracer, offset, fraction, jnp.asarray(matrix), jnp.asarray(twiddle))
    block = pl.BlockSpec((SUB, rows, cells), lambda g: (g, 0, 0))
    return pl.pallas_call(
        write_out,
        out_shape=jax.ShapeDtypeStruct(tracer.shape, jnp.float32),
        grid=(channels // SUB,),
        in_specs=[block],
        out_specs=block,
        compiler_params=pltpu.CompilerParams(vmem_limit_bytes=VMEM_LIMIT),
        cost_estimate=pl.CostEstimate(flops=0, bytes_accessed=4 * 10**6, transcendentals=0),
    )(result)


def solution(mesh):
    placed = (P(None, "lat", "lon"), P("lat", "lon"), P("lat", "lon"), P("lat", "lon"), P())
    step = functools.partial(body, mesh.shape["lat"], mesh.shape["lon"])
    return jax.shard_map(
        step, mesh=mesh, in_specs=placed, out_specs=P(None, "lat", "lon"), check_vma=False
    )
```

```python
import functools
import math

import jax
import jax.numpy as jnp
import numpy as np
from jax import lax
from jax.experimental import pallas as pl
from jax.experimental.pallas import tpu as pltpu
from jax.sharding import PartitionSpec as P

NLON = 2048
BLK = 128
HL = 2
PROWS = 8
NBLK = NLON // BLK
SUB = 8
HALF = NBLK // 2 + 1
MESH = pl.DeviceIdType.MESH
VMEM_LIMIT = 48 * 2**20


def dft_tables():
    lanes = np.arange(BLK)
    angles = 2.0 * math.pi * (np.outer(lanes, lanes) % BLK) / BLK
    cosines, sines = np.cos(angles), np.sin(angles)
    matrix = np.block([[cosines, -sines], [sines, cosines]])
    turns = 2.0 * math.pi * np.outer(np.arange(NBLK), lanes) / NLON
    twiddle = np.stack([np.cos(turns), np.sin(turns)])
    return matrix.astype(np.float32), twiddle.astype(np.float32)


def add(left, right):
    if left is None:
        return right
    return left if right is None else left + right


def sub(left, right):
    if right is None:
        return left
    return -right if left is None else left - right


def scaled(value, factor):
    return None if value is None or factor == 0.0 else value * factor


def turned(value, cosine, sine):
    re, im = value
    cosine, sine = (0.0 if abs(v) < 1e-12 else v for v in (cosine, sine))
    if sine == 0.0 and cosine == 1.0:
        return value
    if cosine == 0.0 and abs(sine) == 1.0:
        if sine > 0:
            return (None if im is None else -im), re
        return im, (None if re is None else -re)
    return sub(scaled(re, cosine), scaled(im, sine)), add(scaled(re, sine), scaled(im, cosine))


def fourier(values, sign):
    count = len(values)
    if count == 1:
        return values
    even, odd = fourier(values[::2], sign), fourier(values[1::2], sign)
    low, high = [], []
    for k in range(count // 2):
        angle = sign * 2.0 * math.pi * k / count
        re, im = turned(odd[k], math.cos(angle), math.sin(angle))
        low.append((add(even[k][0], re), add(even[k][1], im)))
        high.append((sub(even[k][0], re), sub(even[k][1], im)))
    return low + high


def weights_of(t):
    return (
        -t * (t - 1.0) * (t - 2.0) / 6.0,
        (t + 1.0) * (t - 1.0) * (t - 2.0) / 2.0,
        -(t + 1.0) * t * (t - 2.0) / 2.0,
        (t + 1.0) * t * (t - 1.0) / 6.0,
    )


def halves(values):
    upper = values.astype(jnp.bfloat16)
    return upper, (values - upper.astype(jnp.float32)).astype(jnp.bfloat16)


def wide(row):
    return jnp.broadcast_to(row, (SUB, BLK))


def lanes_at(values, index):
    return jnp.take_along_axis(values, index, axis=1, mode="promise_in_bounds")


def row_of(values, row):
    index = jnp.full((SUB, BLK), row, jnp.int32)
    return jnp.take_along_axis(values, index, axis=0, mode="promise_in_bounds")


def cubic_limited(values, anchor, weights):
    before = lanes_at(values, anchor - 1)
    here = lanes_at(values, anchor)
    after = lanes_at(values, anchor + 1)
    beyond = lanes_at(values, anchor + 2)
    mixed = weights[0] * before + weights[1] * here + weights[2] * after + weights[3] * beyond
    return jnp.minimum(jnp.maximum(mixed, jnp.minimum(here, after)), jnp.maximum(here, after))


def lanes(block):
    return pl.ds(pl.multiple_of(block * BLK, BLK), BLK)


def kernel(
    n_lat, n_lon, src_h, cut_h, trc_h, off_h, frac_h, mat_h, twd_h, out,
    src_s, cut_s, trc, off, frac, mat, twd,
    mid, side_0, side_1, side_2, side_3, ring, ids, ids_out, fracs, ids_s, coef, anch, damp, lim, spec, done, back,
    halo_send, halo_recv, pol_send, pol_recv, idx_send, idx_recv, frc_send, frc_recv,
    ret_send, ret_recv, loc_sem,
):
    sides = (side_0, side_1, side_2, side_3)
    channels, rows, cells = trc.shape
    nb = cells // BLK
    groups = channels // SUB
    shares = n_lon // groups
    work_rows = PROWS // shares
    tall = work_rows * SUB
    lat, lon = lax.axis_index("lat"), lax.axis_index("lon")
    first_row = lat * rows
    first_block = lon * nb
    right, left = lax.rem(lon + 1, n_lon), lax.rem(lon + n_lon - 1, n_lon)
    down, up = lax.rem(lat + 1, n_lat), lax.rem(lat + n_lat - 1, n_lat)
    polar = (lat == 0) | (lat == n_lat - 1)
    slab = jnp.where(lat == 0, 0, rows - PROWS)
    worker = (lat == 2) | (lat == n_lat - 3)
    northern = lat < n_lat // 2
    mate = jnp.where(northern, 2 - lat, 2 * n_lat - 4 - lat)
    pole = jnp.where(northern, 0, 1)
    peers = [lax.rem(lon + d, n_lon) for d in range(n_lon)]

    edges = sorted({0, nb - 1})
    middle = list(range(1, nb - 1))

    def local(src, dst, sem):
        return pltpu.make_async_copy(src, dst, loc_sem.at[sem])

    def block_span(first_block_in, count):
        return pl.ds(first_block_in * BLK, count * BLK)

    loads = [
        local(trc_h.at[:, :, block_span(b, 1)], trc.at[:, :, block_span(b, 1)], n)
        for n, b in enumerate(edges)
    ]
    small = [local(off_h, off, 2), local(frac_h, frac, 3), local(src_h, src_s, 4)]
    tables = [local(cut_h, cut_s, 5), local(mat_h, mat, 6), local(twd_h, twd, 7)]
    for copy in loads:
        copy.start()
    centre = []
    if middle:
        span = block_span(1, len(middle))
        centre = [local(trc_h.at[:, :, span], trc.at[:, :, span], 8)]
    for copy in small + centre:
        copy.start()

    @pl.when(worker)
    def _():
        for copy in tables:
            copy.start()

    barrier = pltpu.get_barrier_semaphore()
    for device in ((lat, left), (lat, right), (up, lon), (down, lon)):
        pl.semaphore_signal(barrier, inc=1, device_id=device, device_id_type=MESH)

    @pl.when(polar | worker)
    def _():
        for peer in peers:
            pl.semaphore_signal(barrier, inc=1, device_id=(mate, peer), device_id_type=MESH)

    def turn(blocks, row_groups, skip_pole):
        @pl.loop(0, groups * len(row_groups))
        def _(step):
            ch = pl.multiple_of(lax.rem(step, groups) * SUB, SUB)
            index = lax.div(step, groups)
            row = pl.multiple_of(index * SUB if len(row_groups) > 1 else row_groups[0], SUB)

            def move():
                for b in blocks:
                    tile = trc[pl.ds(ch, SUB), pl.ds(row, SUB), b * BLK : (b + 1) * BLK]
                    mid[pl.ds(HL + row, SUB), b, pl.ds(ch, SUB), :] = jnp.swapaxes(tile, 0, 1)

            if skip_pole:
                pl.when(jnp.logical_not(polar & (row == slab)))(move)
            else:
                move()

    every = range(rows // SUB)
    for copy in loads:
        copy.wait()

    @pl.when(polar)
    def _():
        for copy in centre:
            copy.wait()
        turn(edges + middle, [slab], False)

    @pl.when(jnp.logical_not(polar))
    def _():
        turn(edges, every, False)

    pl.semaphore_wait(barrier, jnp.where(polar | worker, 4 + n_lon, 4))

    def group_of(place):
        return pl.multiple_of(lax.rem(place, groups) * SUB, SUB)

    def span_of(place):
        return pl.ds(place * nb, nb)

    def remote(src, dst, send, recv, device):
        return pltpu.make_async_remote_copy(
            src_ref=src, dst_ref=dst, send_sem=send, recv_sem=recv,
            device_id=device, device_id_type=MESH,
        )

    slab_at = pl.ds(pl.multiple_of(slab, SUB), PROWS)
    own = span_of(lon)
    ring_copies, back_copies = [], []
    for d, peer in enumerate(peers):
        ring_copies += [
            remote(ids_out, ids.at[lon], idx_send.at[d], idx_recv.at[d], (mate, peer)),
            remote(frac.at[slab_at], fracs.at[lon], frc_send.at[d], frc_recv.at[d], (mate, peer)),
            remote(
                mid.at[pl.ds(HL + slab, PROWS), :, pl.ds(group_of(peer), SUB), :],
                ring.at[:, own],
                pol_send.at[d], pol_recv.at[d], (mate, peer),
            ),
        ]
        back_copies.append(
            remote(
                done.at[:, span_of(peer)],
                back.at[
                    pl.ds(lax.div(lon, groups) * work_rows, work_rows), :, pl.ds(group_of(lon), SUB), :
                ],
                ret_send.at[d], ret_recv.at[d], (mate, peer),
            )
        )

    first, last = 0, nb - 1
    top, bottom = pl.ds(HL, HL), pl.ds(rows, HL)
    over, under = pl.ds(0, HL), pl.ds(HL + rows, HL)
    inner = pl.ds(2 * HL, rows - 2 * HL)
    some = pl.ds(jnp.where(lat == 0, PROWS, 2 * HL), rows - PROWS)
    has_up, has_down = lat > 0, lat < n_lat - 1
    counter = iter(range(100))

    def halo(src, dst, device):
        n = next(counter)
        return remote(src, dst, halo_send.at[n], halo_recv.at[n], device)

    lat_halos = [
        (has_down, has_up, halo(mid.at[bottom], mid.at[over], (down, lon))),
        (has_up, has_down, halo(mid.at[top], mid.at[under], (up, lon))),
    ]
    lon_halos, rims, passed = [], [], []
    for g in range(groups):
        chans, side = pl.ds(g * SUB, SUB), sides[g]
        copies = []
        for to, block, half in ((right, last, 0), (left, first, 1)):
            n = next(counter)
            for span, when in ((inner, jnp.logical_not(polar)), (some, polar)):
                copies.append((when, when, remote(
                    mid.at[span, block, chans], side.at[half, span],
                    halo_send.at[n], halo_recv.at[n], (lat, to),
                )))
            for span, when in ((top, has_up), (bottom, has_down)):
                rims.append((when, when, halo(
                    mid.at[span, block, chans], side.at[half, span], (lat, to))))
            forward = [
                (has_down, has_up, halo(side.at[half, bottom], side.at[half, over], (down, lon))),
                (has_up, has_down, halo(side.at[half, top], side.at[half, under], (up, lon))),
            ]
            passed += forward
            copies += forward
        lon_halos.append(copies)

    def gated(condition, action):
        @pl.when(condition)
        def _():
            action()

    for copy in small:
        copy.wait()

    @pl.when(polar)
    def _():
        ids_out[0:PROWS] = off[slab_at]
        placed = jnp.zeros((PROWS, BLK), jnp.int32)
        row_ids = lax.broadcasted_iota(jnp.int32, (PROWS, BLK), 0)
        lane_ids = lax.broadcasted_iota(jnp.int32, (PROWS, BLK), 1)
        for j in range(PROWS):
            for b in range(nb):
                placed = jnp.where((row_ids == j) & (lane_ids == b), src_s[b, slab + j], placed)
        ids_out[PROWS : 2 * PROWS, 0:BLK] = placed
        if nb > 1:
            ids_out[PROWS : 2 * PROWS, BLK:] = jnp.zeros((PROWS, cells - BLK), jnp.int32)
        for copy in ring_copies:
            copy.start()
        turn(edges + middle, every, True)

    def send_group(g):
        for sends, _, copy in lon_halos[g]:
            if all(copy is not other for _, _, other in passed):
                gated(sends, copy.start)

    for sends, _, copy in rims:
        gated(sends, copy.start)
    ahead = groups
    for g in range(ahead):
        send_group(g)

    @pl.when(jnp.logical_not(polar))
    def _():
        for copy in centre:
            copy.wait()
        if middle:
            turn(middle, every, False)

    for sends, _, copy in lat_halos:
        gated(sends, copy.start)

    def tile(group, b, edge, chosen):
        row = pl.multiple_of(group * SUB, SUB)
        at = lanes(b)
        weights = weights_of(frac[pl.ds(row, SUB), at])
        anchors = off[pl.ds(row, SUB), at]
        results = {g: [] for g in chosen}
        for j in range(SUB):
            block_id = src_s[b, row + j]
            source_row = lax.div(block_id, NBLK) - first_row + HL
            source_row = jnp.clip(source_row, 0, rows + 2 * HL - 1)
            place = lax.rem(lax.rem(block_id, NBLK) - first_block + 1 + NBLK, NBLK)
            near = jnp.clip(place - 1, 0, nb - 1)
            far = jnp.minimum(place, 1)
            spot = jnp.full((SUB, BLK), place, jnp.int32)
            inside = (spot >= 1) & (spot <= nb)
            anchor = wide(anchors[j : j + 1])
            factors = [wide(w[j : j + 1]) for w in weights]
            for g in chosen:
                values = mid[source_row, near, pl.ds(g * SUB, SUB), :]
                if edge:
                    values = jnp.where(inside, values, sides[g][far, source_row])
                results[g].append(cubic_limited(values, anchor, factors))
        for g in chosen:
            out[g * SUB : (g + 1) * SUB, pl.ds(row, SUB), at] = jnp.swapaxes(
                jnp.stack(results[g]), 0, 1
            )

    tiles = rows // SUB

    def sweep(blocks, edge, chosen):
        count = len(blocks)
        if not count:
            return
        start, stride = blocks[0], (blocks[1] - blocks[0] if count > 1 else 1)

        @pl.loop(0, tiles * count)
        def _(step):
            group = lax.div(step, count)
            at_pole = ((lat == 0) & (group == 0)) | ((lat == n_lat - 1) & (group == tiles - 1))

            @pl.when(jnp.logical_not(at_pole))
            def _():
                tile(group, start + stride * lax.rem(step, count), edge, chosen)

    for _, receives, copy in rims:
        gated(receives, copy.wait_recv)
    for sends, _, copy in passed:
        gated(sends, copy.start)
    for _, receives, copy in lat_halos:
        gated(receives, copy.wait_recv)
    sweep(middle, False, range(groups))

    @pl.when(worker)
    def _():
        for copy in tables:
            copy.wait()
        for n in range(0, len(ring_copies), 3):
            ring_copies[n].wait_recv()
            ring_copies[n + 1].wait_recv()
        fetch = pltpu.make_async_copy(
            ids.at[:, pl.ds(PROWS, PROWS), pl.ds(0, BLK)], ids_s, loc_sem.at[9]
        )
        fetch.start()
        row_base = lax.div(lon, groups) * work_rows
        slab_global = jnp.where(northern, 0, n_lat * rows - PROWS)

        @pl.loop(0, work_rows)
        def _(j):
            jw = row_base + j
            for b in range(NBLK):
                q, at = b // nb, pl.ds(b % nb * BLK, BLK)
                for n, weight in enumerate(weights_of(row_of(fracs[q, :, at], jw))):
                    coef[j, b, n] = weight
                anch[j, b] = row_of(ids[q, 0:PROWS, at], jw)
            kappa = cut_s[pole, jw].astype(jnp.float32)
            for k in range(HALF):
                wave = k + NBLK * lax.broadcasted_iota(jnp.int32, (SUB, BLK), 1)
                wave = jnp.minimum(wave, NLON - wave)
                kept = (wave >= 1) & (wave < NLON // 2)
                damping = 1.0 - kappa / jnp.maximum(wave, 1).astype(jnp.float32)
                damp[j, k] = jnp.where(kept, jnp.maximum(damping, 0.0), 0.0) * (1.0 / NLON)

        fetch.wait()
        for n in range(2, len(ring_copies), 3):
            ring_copies[n].wait_recv()

        @pl.loop(0, work_rows)
        def _(j):
            jw = row_base + j
            band = []
            for b in range(NBLK):
                q, bb = b // nb, b % nb
                block_id = ids_s[q, jw, bb]
                source_row = jnp.clip(lax.div(block_id, NBLK) - slab_global, 0, PROWS - 1)
                values = ring[source_row, lax.rem(block_id, NBLK)]
                limited = cubic_limited(values, anch[j, b], [coef[j, b, n] for n in range(4)])
                lim[j, b] = limited
                band.append((limited, None))
            waves = fourier(band, -1)
            for k in range(HALF):
                re, im = waves[k]
                cosine, sine = wide(twd[0, k : k + 1, :]), wide(twd[1, k : k + 1, :])
                at = pl.ds(pl.multiple_of(k * tall + j * SUB, SUB), SUB)
                if im is None:
                    spec[at, 0:BLK] = re * cosine
                    spec[at, BLK : 2 * BLK] = -re * sine
                else:
                    spec[at, 0:BLK] = re * cosine + im * sine
                    spec[at, BLK : 2 * BLK] = im * cosine - re * sine

        def transform():
            upper, lower = halves(spec[...])
            mat_upper, mat_lower = halves(mat[...])
            product = functools.partial(jnp.dot, preferred_element_type=jnp.float32)
            spec[...] = product(upper, mat_upper) + (
                product(lower, mat_upper) + product(upper, mat_lower)
            )

        transform()

        @pl.loop(0, work_rows)
        def _(j):
            for k in range(HALF):
                damping = damp[j, k]
                at = pl.ds(pl.multiple_of(k * tall + j * SUB, SUB), SUB)
                spec[at, 0:BLK] = spec[at, 0:BLK] * damping
                spec[at, BLK : 2 * BLK] = -spec[at, BLK : 2 * BLK] * damping

        transform()

        @pl.loop(0, work_rows)
        def _(j):
            waves = []
            for k in range(HALF):
                at = pl.ds(pl.multiple_of(k * tall + j * SUB, SUB), SUB)
                re, im = spec[at, 0:BLK], spec[at, BLK : 2 * BLK]
                cosine, sine = wide(twd[0, k : k + 1, :]), wide(twd[1, k : k + 1, :])
                real = re * cosine + im * sine
                waves.append((real, None if k in (0, HALF - 1) else re * sine - im * cosine))
            for k in range(HALF, NBLK):
                re, im = waves[NBLK - k]
                waves.append((re, -im))
            removed = fourier(waves, 1)
            for b in range(NBLK):
                done[j, b] = lim[j, b] - removed[b][0]

        for copy in back_copies:
            copy.start()

    for g, copies in enumerate(lon_halos):
        for _, receives, copy in copies:
            gated(receives, copy.wait_recv)
        if g + ahead < groups:
            send_group(g + ahead)
        sweep(edges, True, [g])

    @pl.when(polar)
    def _():
        for copy in back_copies:
            copy.wait_recv()

        @pl.loop(0, groups)
        def _(g):
            ch = pl.multiple_of(g * SUB, SUB)
            for b in range(nb):
                at = slice(b * BLK, (b + 1) * BLK)
                out[pl.ds(ch, SUB), slab_at, at] = jnp.swapaxes(back[:, b, pl.ds(ch, SUB), :], 0, 1)

        for copy in ring_copies:
            copy.wait_send()

    @pl.when(worker)
    def _():
        for copy in back_copies:
            copy.wait_send()

    for sends, _, copy in lat_halos + rims + sum(lon_halos, []):
        gated(sends, copy.wait_send)


def body(n_lat, n_lon, tracer, source, offset, fraction, cutoffs):
    channels, rows, cells = tracer.shape
    shares = n_lon // (channels // SUB)
    work_rows = PROWS // shares
    matrix, twiddle = dft_tables()
    operands = (
        source.T, cutoffs, tracer, offset, fraction, jnp.asarray(matrix), jnp.asarray(twiddle)
    )
    dma = pltpu.SemaphoreType.DMA
    vmem = pl.BlockSpec(memory_space=pltpu.VMEM)
    return pl.pallas_call(
        functools.partial(kernel, n_lat, n_lon),
        out_shape=jax.ShapeDtypeStruct(tracer.shape, jnp.float32),
        in_specs=[pl.BlockSpec(memory_space=pltpu.HBM)] * 7,
        out_specs=vmem,
        scratch_shapes=[
            pltpu.SMEM(source.shape[::-1], jnp.int32),
            pltpu.SMEM(cutoffs.shape, jnp.int32),
            pltpu.VMEM(tracer.shape, jnp.float32),
            pltpu.VMEM(offset.shape, jnp.int32),
            pltpu.VMEM(fraction.shape, jnp.float32),
            pltpu.VMEM(matrix.shape, jnp.float32),
            pltpu.VMEM(twiddle.shape, jnp.float32),
            pltpu.VMEM((rows + 2 * HL, cells // BLK, channels, BLK), jnp.float32),
        ] + [pltpu.VMEM((2, rows + 2 * HL, SUB, BLK), jnp.float32)] * 4 + [
            pltpu.VMEM((PROWS, NBLK, SUB, BLK), jnp.float32),
            pltpu.VMEM((n_lon, 2 * PROWS, cells), jnp.int32),
            pltpu.VMEM((2 * PROWS, cells), jnp.int32),
            pltpu.VMEM((n_lon, PROWS, cells), jnp.float32),
            pltpu.SMEM((n_lon, PROWS, BLK), jnp.int32),
            pltpu.VMEM((work_rows, NBLK, 4, SUB, BLK), jnp.float32),
            pltpu.VMEM((work_rows, NBLK, SUB, BLK), jnp.int32),
            pltpu.VMEM((work_rows, HALF, SUB, BLK), jnp.float32),
            pltpu.VMEM((work_rows, NBLK, SUB, BLK), jnp.float32),
            pltpu.VMEM((HALF * work_rows * SUB, 2 * BLK), jnp.float32),
            pltpu.VMEM((work_rows, NBLK, SUB, BLK), jnp.float32),
            pltpu.VMEM((PROWS, cells // BLK, channels, BLK), jnp.float32),
            dma((42,)), dma((42,)),
        ] + [dma((n_lon,))] * 8 + [dma((10,))],
        compiler_params=pltpu.CompilerParams(
            collective_id=0, has_side_effects=True, vmem_limit_bytes=VMEM_LIMIT
        ),
        cost_estimate=pl.CostEstimate(flops=10**9, bytes_accessed=5 * 10**6, transcendentals=0),
    )(*(pltpu.with_memory_space_constraint(value, pltpu.HBM) for value in operands))


def solution(mesh):
    placed = (P(None, "lat", "lon"), P("lat", "lon"), P("lat", "lon"), P("lat", "lon"), P())
    step = functools.partial(body, mesh.shape["lat"], mesh.shape["lon"])
    return jax.shard_map(
        step, mesh=mesh, in_specs=placed, out_specs=P(None, "lat", "lon"), check_vma=False
    )
```

```python
import functools
import math

import jax
import jax.numpy as jnp
import numpy as np
from jax import lax
from jax.experimental import pallas as pl
from jax.experimental.pallas import tpu as pltpu
from jax.sharding import PartitionSpec as P

NLON = 2048
BLK = 128
HL = 2
PROWS = 8
NBLK = NLON // BLK
SUB = 8
HALF = NBLK // 2 + 1
PARTS = 2
MESH = pl.DeviceIdType.MESH
VMEM_LIMIT = 48 * 2**20


def dft_tables():
    lanes = np.arange(BLK)
    angles = 2.0 * math.pi * (np.outer(lanes, lanes) % BLK) / BLK
    cosines, sines = np.cos(angles), np.sin(angles)
    matrix = np.block([[cosines, -sines], [sines, cosines]])
    turns = 2.0 * math.pi * np.outer(np.arange(NBLK), lanes) / NLON
    twiddle = np.stack([np.cos(turns), np.sin(turns)])
    return matrix.astype(np.float32), twiddle.astype(np.float32)


def add(left, right):
    if left is None:
        return right
    return left if right is None else left + right


def sub(left, right):
    if right is None:
        return left
    return -right if left is None else left - right


def scaled(value, factor):
    return None if value is None or factor == 0.0 else value * factor


def turned(value, cosine, sine):
    re, im = value
    cosine, sine = (0.0 if abs(v) < 1e-12 else v for v in (cosine, sine))
    if sine == 0.0 and cosine == 1.0:
        return value
    if cosine == 0.0 and abs(sine) == 1.0:
        if sine > 0:
            return (None if im is None else -im), re
        return im, (None if re is None else -re)
    return sub(scaled(re, cosine), scaled(im, sine)), add(scaled(re, sine), scaled(im, cosine))


def fourier(values, sign):
    count = len(values)
    if count == 1:
        return values
    even, odd = fourier(values[::2], sign), fourier(values[1::2], sign)
    low, high = [], []
    for k in range(count // 2):
        angle = sign * 2.0 * math.pi * k / count
        re, im = turned(odd[k], math.cos(angle), math.sin(angle))
        low.append((add(even[k][0], re), add(even[k][1], im)))
        high.append((sub(even[k][0], re), sub(even[k][1], im)))
    return low + high


def weights_of(t):
    return (
        -t * (t - 1.0) * (t - 2.0) / 6.0,
        (t + 1.0) * (t - 1.0) * (t - 2.0) / 2.0,
        -(t + 1.0) * t * (t - 2.0) / 2.0,
        (t + 1.0) * t * (t - 1.0) / 6.0,
    )


def halves(values):
    upper = values.astype(jnp.bfloat16)
    return upper, (values - upper.astype(jnp.float32)).astype(jnp.bfloat16)


def wide(row):
    return jnp.broadcast_to(row, (SUB, BLK))


def lanes_at(values, index):
    return jnp.take_along_axis(values, index, axis=1, mode="promise_in_bounds")


def row_of(values, row):
    index = jnp.full((SUB, BLK), row, jnp.int32)
    return jnp.take_along_axis(values, index, axis=0, mode="promise_in_bounds")


def cubic_limited(values, anchor, weights):
    before = lanes_at(values, anchor - 1)
    here = lanes_at(values, anchor)
    after = lanes_at(values, anchor + 1)
    beyond = lanes_at(values, anchor + 2)
    mixed = weights[0] * before + weights[1] * here + weights[2] * after + weights[3] * beyond
    return jnp.minimum(jnp.maximum(mixed, jnp.minimum(here, after)), jnp.maximum(here, after))


def lanes(block):
    return pl.ds(pl.multiple_of(block * BLK, BLK), BLK)


def kernel(
    n_lat, n_lon, src_h, cut_h, trc_h, off_h, frac_h, mat_h, twd_h, out,
    src_s, cut_s, trc, off, frac, mat, twd,
    mid, side_0, side_1, side_2, side_3, ring, ids, ids_out, fracs, ids_s, coef, anch, damp, lim, spec, done, back,
    halo_send, halo_recv, pol_send, pol_recv, idx_send, idx_recv, frc_send, frc_recv,
    ret_send, ret_recv, loc_sem,
):
    sides = (side_0, side_1, side_2, side_3)
    channels, rows, cells = trc.shape
    nb = cells // BLK
    groups = channels // SUB
    shares = n_lon // groups
    work_rows = PROWS // shares
    part_rows = work_rows // PARTS
    tall = part_rows * SUB
    lat, lon = lax.axis_index("lat"), lax.axis_index("lon")
    first_row = lat * rows
    first_block = lon * nb
    right, left = lax.rem(lon + 1, n_lon), lax.rem(lon + n_lon - 1, n_lon)
    down, up = lax.rem(lat + 1, n_lat), lax.rem(lat + n_lat - 1, n_lat)
    polar = (lat == 0) | (lat == n_lat - 1)
    slab = jnp.where(lat == 0, 0, rows - PROWS)
    worker = (lat == 2) | (lat == n_lat - 3)
    northern = lat < n_lat // 2
    mate = jnp.where(northern, 2 - lat, 2 * n_lat - 4 - lat)
    pole = jnp.where(northern, 0, 1)
    peers = [lax.rem(lon + d, n_lon) for d in range(n_lon)]

    edges = sorted({0, nb - 1})
    middle = list(range(1, nb - 1))

    def local(src, dst, sem):
        return pltpu.make_async_copy(src, dst, loc_sem.at[sem])

    def block_span(first_block_in, count):
        return pl.ds(first_block_in * BLK, count * BLK)

    loads = [
        local(trc_h.at[:, :, block_span(b, 1)], trc.at[:, :, block_span(b, 1)], n)
        for n, b in enumerate(edges)
    ]
    small = [local(off_h, off, 2), local(frac_h, frac, 3), local(src_h, src_s, 4)]
    tables = [local(cut_h, cut_s, 5), local(mat_h, mat, 6), local(twd_h, twd, 7)]
    for copy in loads:
        copy.start()
    centre = []
    if middle:
        span = block_span(1, len(middle))
        centre = [local(trc_h.at[:, :, span], trc.at[:, :, span], 8)]
    for copy in small + centre:
        copy.start()

    @pl.when(worker)
    def _():
        for copy in tables:
            copy.start()

    barrier = pltpu.get_barrier_semaphore()
    for device in ((lat, left), (lat, right), (up, lon), (down, lon)):
        pl.semaphore_signal(barrier, inc=1, device_id=device, device_id_type=MESH)

    @pl.when(polar | worker)
    def _():
        for peer in peers:
            pl.semaphore_signal(barrier, inc=1, device_id=(mate, peer), device_id_type=MESH)

    def turn(blocks, row_groups, skip_pole):
        @pl.loop(0, groups * len(row_groups))
        def _(step):
            ch = pl.multiple_of(lax.rem(step, groups) * SUB, SUB)
            index = lax.div(step, groups)
            row = pl.multiple_of(index * SUB if len(row_groups) > 1 else row_groups[0], SUB)

            def move():
                for b in blocks:
                    tile = trc[pl.ds(ch, SUB), pl.ds(row, SUB), b * BLK : (b + 1) * BLK]
                    mid[pl.ds(HL + row, SUB), b, pl.ds(ch, SUB), :] = jnp.swapaxes(tile, 0, 1)

            if skip_pole:
                pl.when(jnp.logical_not(polar & (row == slab)))(move)
            else:
                move()

    every = range(rows // SUB)
    for copy in loads:
        copy.wait()

    @pl.when(polar)
    def _():
        for copy in centre:
            copy.wait()
        turn(edges + middle, [slab], False)

    @pl.when(jnp.logical_not(polar))
    def _():
        turn(edges, every, False)

    pl.semaphore_wait(barrier, jnp.where(polar | worker, 4 + n_lon, 4))

    def group_of(place):
        return pl.multiple_of(lax.rem(place, groups) * SUB, SUB)

    def span_of(place):
        return pl.ds(place * nb, nb)

    def remote(src, dst, send, recv, device):
        return pltpu.make_async_remote_copy(
            src_ref=src, dst_ref=dst, send_sem=send, recv_sem=recv,
            device_id=device, device_id_type=MESH,
        )

    slab_at = pl.ds(pl.multiple_of(slab, SUB), PROWS)
    own = span_of(lon)
    ring_copies, back_copies = [], []
    for d, peer in enumerate(peers):
        ring_copies += [
            remote(ids_out, ids.at[lon], idx_send.at[d], idx_recv.at[d], (mate, peer)),
            remote(frac.at[slab_at], fracs.at[lon], frc_send.at[d], frc_recv.at[d], (mate, peer)),
            remote(
                mid.at[pl.ds(HL + slab, PROWS), :, pl.ds(group_of(peer), SUB), :],
                ring.at[:, own],
                pol_send.at[d], pol_recv.at[d], (mate, peer),
            ),
        ]

    for part in range(PARTS):
        for d, peer in enumerate(peers):
            to_row = lax.div(lon, groups) * work_rows + part * part_rows
            back_copies.append(
                remote(
                    done.at[pl.ds(part * part_rows, part_rows), span_of(peer)],
                    back.at[pl.ds(to_row, part_rows), :, pl.ds(group_of(lon), SUB), :],
                    ret_send.at[part * n_lon + d], ret_recv.at[part * n_lon + d], (mate, peer),
                )
            )

    first, last = 0, nb - 1
    top, bottom = pl.ds(HL, HL), pl.ds(rows, HL)
    over, under = pl.ds(0, HL), pl.ds(HL + rows, HL)
    inner = pl.ds(2 * HL, rows - 2 * HL)
    some = pl.ds(jnp.where(lat == 0, PROWS, 2 * HL), rows - PROWS)
    has_up, has_down = lat > 0, lat < n_lat - 1
    counter = iter(range(100))

    def halo(src, dst, device):
        n = next(counter)
        return remote(src, dst, halo_send.at[n], halo_recv.at[n], device)

    lat_halos = [
        (has_down, has_up, halo(mid.at[bottom], mid.at[over], (down, lon))),
        (has_up, has_down, halo(mid.at[top], mid.at[under], (up, lon))),
    ]
    lon_halos, rims, passed = [], [], []
    for g in range(groups):
        chans, side = pl.ds(g * SUB, SUB), sides[g]
        copies = []
        for to, block, half in ((right, last, 0), (left, first, 1)):
            n = next(counter)
            for span, when in ((inner, jnp.logical_not(polar)), (some, polar)):
                copies.append((when, when, remote(
                    mid.at[span, block, chans], side.at[half, span],
                    halo_send.at[n], halo_recv.at[n], (lat, to),
                )))
            for span, when in ((top, has_up), (bottom, has_down)):
                rims.append((when, when, halo(
                    mid.at[span, block, chans], side.at[half, span], (lat, to))))
            forward = [
                (has_down, has_up, halo(side.at[half, bottom], side.at[half, over], (down, lon))),
                (has_up, has_down, halo(side.at[half, top], side.at[half, under], (up, lon))),
            ]
            passed += forward
            copies += forward
        lon_halos.append(copies)

    def gated(condition, action):
        @pl.when(condition)
        def _():
            action()

    for copy in small:
        copy.wait()

    @pl.when(polar)
    def _():
        ids_out[0:PROWS] = off[slab_at]
        placed = jnp.zeros((PROWS, BLK), jnp.int32)
        row_ids = lax.broadcasted_iota(jnp.int32, (PROWS, BLK), 0)
        lane_ids = lax.broadcasted_iota(jnp.int32, (PROWS, BLK), 1)
        for j in range(PROWS):
            for b in range(nb):
                placed = jnp.where((row_ids == j) & (lane_ids == b), src_s[b, slab + j], placed)
        ids_out[PROWS : 2 * PROWS, 0:BLK] = placed
        if nb > 1:
            ids_out[PROWS : 2 * PROWS, BLK:] = jnp.zeros((PROWS, cells - BLK), jnp.int32)
        for copy in ring_copies:
            copy.start()
        turn(edges + middle, every, True)

    def send_lon(only_polar):
        for copies in lon_halos:
            for sends, _, copy in copies:
                if all(copy is not other for _, _, other in passed) and (sends is polar) == only_polar:
                    gated(sends, copy.start)

    for sends, _, copy in rims:
        gated(sends, copy.start)
    send_lon(False)

    @pl.when(jnp.logical_not(polar))
    def _():
        for copy in centre:
            copy.wait()
        if middle:
            turn(middle, every, False)

    for sends, _, copy in lat_halos:
        gated(sends, copy.start)

    def tile(group, b, edge, chosen):
        row = pl.multiple_of(group * SUB, SUB)
        at = lanes(b)
        weights = weights_of(frac[pl.ds(row, SUB), at])
        anchors = off[pl.ds(row, SUB), at]
        results = {g: [] for g in chosen}
        for j in range(SUB):
            block_id = src_s[b, row + j]
            source_row = lax.div(block_id, NBLK) - first_row + HL
            source_row = jnp.clip(source_row, 0, rows + 2 * HL - 1)
            place = lax.rem(lax.rem(block_id, NBLK) - first_block + 1 + NBLK, NBLK)
            near = jnp.clip(place - 1, 0, nb - 1)
            far = jnp.minimum(place, 1)
            spot = jnp.full((SUB, BLK), place, jnp.int32)
            inside = (spot >= 1) & (spot <= nb)
            anchor = wide(anchors[j : j + 1])
            factors = [wide(w[j : j + 1]) for w in weights]
            for g in chosen:
                values = mid[source_row, near, pl.ds(g * SUB, SUB), :]
                if edge:
                    values = jnp.where(inside, values, sides[g][far, source_row])
                results[g].append(cubic_limited(values, anchor, factors))
        for g in chosen:
            out[g * SUB : (g + 1) * SUB, pl.ds(row, SUB), at] = jnp.swapaxes(
                jnp.stack(results[g]), 0, 1
            )

    tiles = rows // SUB

    def sweep(blocks, edge, chosen):
        count = len(blocks)
        if not count:
            return
        start, stride = blocks[0], (blocks[1] - blocks[0] if count > 1 else 1)

        @pl.loop(0, tiles * count)
        def _(step):
            group = lax.div(step, count)
            at_pole = ((lat == 0) & (group == 0)) | ((lat == n_lat - 1) & (group == tiles - 1))

            @pl.when(jnp.logical_not(at_pole))
            def _():
                tile(group, start + stride * lax.rem(step, count), edge, chosen)

    for _, receives, copy in rims:
        gated(receives, copy.wait_recv)
    for sends, _, copy in passed:
        gated(sends, copy.start)

    def inner_tiles():
        for _, receives, copy in lat_halos:
            gated(receives, copy.wait_recv)
        sweep(middle, False, range(groups))

    @pl.when(jnp.logical_not(worker))
    def _():
        inner_tiles()

    @pl.when(polar)
    def _():
        for copy in ring_copies:
            copy.wait_send()

    send_lon(True)

    @pl.when(worker)
    def _():
        for copy in tables:
            copy.wait()
        for n in range(0, len(ring_copies), 3):
            ring_copies[n].wait_recv()
            ring_copies[n + 1].wait_recv()
        fetch = pltpu.make_async_copy(
            ids.at[:, pl.ds(PROWS, PROWS), pl.ds(0, BLK)], ids_s, loc_sem.at[9]
        )
        fetch.start()
        row_base = lax.div(lon, groups) * work_rows
        slab_global = jnp.where(northern, 0, n_lat * rows - PROWS)

        @pl.loop(0, work_rows)
        def _(j):
            jw = row_base + j
            for b in range(NBLK):
                q, at = b // nb, pl.ds(b % nb * BLK, BLK)
                for n, weight in enumerate(weights_of(row_of(fracs[q, :, at], jw))):
                    coef[j, b, n] = weight
                anch[j, b] = row_of(ids[q, 0:PROWS, at], jw)
            kappa = cut_s[pole, jw].astype(jnp.float32)
            for k in range(HALF):
                wave = k + NBLK * lax.broadcasted_iota(jnp.int32, (SUB, BLK), 1)
                wave = jnp.minimum(wave, NLON - wave)
                kept = (wave >= 1) & (wave < NLON // 2)
                damping = 1.0 - kappa / jnp.maximum(wave, 1).astype(jnp.float32)
                damp[j, k] = jnp.where(kept, jnp.maximum(damping, 0.0), 0.0) * (1.0 / NLON)

        fetch.wait()
        for n in range(2, len(ring_copies), 3):
            ring_copies[n].wait_recv()

        def transform():
            upper, lower = halves(spec[...])
            mat_upper, mat_lower = halves(mat[...])
            product = functools.partial(jnp.dot, preferred_element_type=jnp.float32)
            spec[...] = product(upper, mat_upper) + (
                product(lower, mat_upper) + product(upper, mat_lower)
            )

        for part in range(PARTS):

            @pl.loop(0, part_rows)
            def _(step):
                j = part * part_rows + step
                jw = row_base + j
                band = []
                for b in range(NBLK):
                    q, bb = b // nb, b % nb
                    block_id = ids_s[q, jw, bb]
                    source_row = jnp.clip(lax.div(block_id, NBLK) - slab_global, 0, PROWS - 1)
                    values = ring[source_row, lax.rem(block_id, NBLK)]
                    limited = cubic_limited(values, anch[j, b], [coef[j, b, n] for n in range(4)])
                    lim[j, b] = limited
                    band.append((limited, None))
                waves = fourier(band, -1)
                for k in range(HALF):
                    re, im = waves[k]
                    cosine, sine = wide(twd[0, k : k + 1, :]), wide(twd[1, k : k + 1, :])
                    at = pl.ds(pl.multiple_of(k * tall + step * SUB, SUB), SUB)
                    if im is None:
                        spec[at, 0:BLK] = re * cosine
                        spec[at, BLK : 2 * BLK] = -re * sine
                    else:
                        spec[at, 0:BLK] = re * cosine + im * sine
                        spec[at, BLK : 2 * BLK] = im * cosine - re * sine

            transform()

            @pl.loop(0, part_rows)
            def _(step):
                j = part * part_rows + step
                for k in range(HALF):
                    damping = damp[j, k]
                    at = pl.ds(pl.multiple_of(k * tall + step * SUB, SUB), SUB)
                    spec[at, 0:BLK] = spec[at, 0:BLK] * damping
                    spec[at, BLK : 2 * BLK] = -spec[at, BLK : 2 * BLK] * damping

            transform()

            @pl.loop(0, part_rows)
            def _(step):
                j = part * part_rows + step
                waves = []
                for k in range(HALF):
                    at = pl.ds(pl.multiple_of(k * tall + step * SUB, SUB), SUB)
                    re, im = spec[at, 0:BLK], spec[at, BLK : 2 * BLK]
                    cosine, sine = wide(twd[0, k : k + 1, :]), wide(twd[1, k : k + 1, :])
                    real = re * cosine + im * sine
                    waves.append((real, None if k in (0, HALF - 1) else re * sine - im * cosine))
                for k in range(HALF, NBLK):
                    re, im = waves[NBLK - k]
                    waves.append((re, -im))
                removed = fourier(waves, 1)
                for b in range(NBLK):
                    done[j, b] = lim[j, b] - removed[b][0]

            for copy in back_copies[part * n_lon : (part + 1) * n_lon]:
                copy.start()

        inner_tiles()

    for g, copies in enumerate(lon_halos):
        for _, receives, copy in copies:
            gated(receives, copy.wait_recv)
        sweep(edges, True, [g])

    @pl.when(polar)
    def _():
        for copy in back_copies:
            copy.wait_recv()

        @pl.loop(0, groups)
        def _(g):
            ch = pl.multiple_of(g * SUB, SUB)
            for b in range(nb):
                at = slice(b * BLK, (b + 1) * BLK)
                out[pl.ds(ch, SUB), slab_at, at] = jnp.swapaxes(back[:, b, pl.ds(ch, SUB), :], 0, 1)

    @pl.when(worker)
    def _():
        for copy in back_copies:
            copy.wait_send()

    for sends, _, copy in lat_halos + rims + sum(lon_halos, []):
        gated(sends, copy.wait_send)


def body(n_lat, n_lon, tracer, source, offset, fraction, cutoffs):
    channels, rows, cells = tracer.shape
    shares = n_lon // (channels // SUB)
    work_rows = PROWS // shares
    matrix, twiddle = dft_tables()
    operands = (
        source.T, cutoffs, tracer, offset, fraction, jnp.asarray(matrix), jnp.asarray(twiddle)
    )
    dma = pltpu.SemaphoreType.DMA
    vmem = pl.BlockSpec(memory_space=pltpu.VMEM)
    return pl.pallas_call(
        functools.partial(kernel, n_lat, n_lon),
        out_shape=jax.ShapeDtypeStruct(tracer.shape, jnp.float32),
        in_specs=[pl.BlockSpec(memory_space=pltpu.HBM)] * 7,
        out_specs=vmem,
        scratch_shapes=[
            pltpu.SMEM(source.shape[::-1], jnp.int32),
            pltpu.SMEM(cutoffs.shape, jnp.int32),
            pltpu.VMEM(tracer.shape, jnp.float32),
            pltpu.VMEM(offset.shape, jnp.int32),
            pltpu.VMEM(fraction.shape, jnp.float32),
            pltpu.VMEM(matrix.shape, jnp.float32),
            pltpu.VMEM(twiddle.shape, jnp.float32),
            pltpu.VMEM((rows + 2 * HL, cells // BLK, channels, BLK), jnp.float32),
        ] + [pltpu.VMEM((2, rows + 2 * HL, SUB, BLK), jnp.float32)] * 4 + [
            pltpu.VMEM((PROWS, NBLK, SUB, BLK), jnp.float32),
            pltpu.VMEM((n_lon, 2 * PROWS, cells), jnp.int32),
            pltpu.VMEM((2 * PROWS, cells), jnp.int32),
            pltpu.VMEM((n_lon, PROWS, cells), jnp.float32),
            pltpu.SMEM((n_lon, PROWS, BLK), jnp.int32),
            pltpu.VMEM((work_rows, NBLK, 4, SUB, BLK), jnp.float32),
            pltpu.VMEM((work_rows, NBLK, SUB, BLK), jnp.int32),
            pltpu.VMEM((work_rows, HALF, SUB, BLK), jnp.float32),
            pltpu.VMEM((work_rows, NBLK, SUB, BLK), jnp.float32),
            pltpu.VMEM((HALF * work_rows // PARTS * SUB, 2 * BLK), jnp.float32),
            pltpu.VMEM((work_rows, NBLK, SUB, BLK), jnp.float32),
            pltpu.VMEM((PROWS, cells // BLK, channels, BLK), jnp.float32),
            dma((42,)), dma((42,)),
        ] + [dma((n_lon,))] * 6 + [dma((PARTS * n_lon,))] * 2 + [dma((10,))],
        compiler_params=pltpu.CompilerParams(
            collective_id=0, has_side_effects=True, vmem_limit_bytes=VMEM_LIMIT
        ),
        cost_estimate=pl.CostEstimate(flops=10**9, bytes_accessed=5 * 10**6, transcendentals=0),
    )(*(pltpu.with_memory_space_constraint(value, pltpu.HBM) for value in operands))


def solution(mesh):
    placed = (P(None, "lat", "lon"), P("lat", "lon"), P("lat", "lon"), P("lat", "lon"), P())
    step = functools.partial(body, mesh.shape["lat"], mesh.shape["lon"])
    return jax.shard_map(
        step, mesh=mesh, in_specs=placed, out_specs=P(None, "lat", "lon"), check_vma=False
    )
```

```python
import functools
import math

import jax
import jax.numpy as jnp
import numpy as np
from jax import lax
from jax.experimental import pallas as pl
from jax.experimental.pallas import tpu as pltpu
from jax.sharding import PartitionSpec as P

NLON = 2048
BLK = 128
HL = 2
PROWS = 8
NBLK = NLON // BLK
SUB = 8
HALF = NBLK // 2 + 1
PARTS = 2
EARLY = 1
MESH = pl.DeviceIdType.MESH
VMEM_LIMIT = 48 * 2**20


def dft_tables():
    lanes = np.arange(BLK)
    angles = 2.0 * math.pi * (np.outer(lanes, lanes) % BLK) / BLK
    cosines, sines = np.cos(angles), np.sin(angles)
    matrix = np.block([[cosines, -sines], [sines, cosines]])
    turns = 2.0 * math.pi * np.outer(np.arange(NBLK), lanes) / NLON
    twiddle = np.stack([np.cos(turns), np.sin(turns)])
    return matrix.astype(np.float32), twiddle.astype(np.float32)


def add(left, right):
    if left is None:
        return right
    return left if right is None else left + right


def sub(left, right):
    if right is None:
        return left
    return -right if left is None else left - right


def scaled(value, factor):
    return None if value is None or factor == 0.0 else value * factor


def turned(value, cosine, sine):
    re, im = value
    cosine, sine = (0.0 if abs(v) < 1e-12 else v for v in (cosine, sine))
    if sine == 0.0 and cosine == 1.0:
        return value
    if cosine == 0.0 and abs(sine) == 1.0:
        if sine > 0:
            return (None if im is None else -im), re
        return im, (None if re is None else -re)
    return sub(scaled(re, cosine), scaled(im, sine)), add(scaled(re, sine), scaled(im, cosine))


def fourier(values, sign):
    count = len(values)
    if count == 1:
        return values
    even, odd = fourier(values[::2], sign), fourier(values[1::2], sign)
    low, high = [], []
    for k in range(count // 2):
        angle = sign * 2.0 * math.pi * k / count
        re, im = turned(odd[k], math.cos(angle), math.sin(angle))
        low.append((add(even[k][0], re), add(even[k][1], im)))
        high.append((sub(even[k][0], re), sub(even[k][1], im)))
    return low + high


def weights_of(t):
    return (
        -t * (t - 1.0) * (t - 2.0) / 6.0,
        (t + 1.0) * (t - 1.0) * (t - 2.0) / 2.0,
        -(t + 1.0) * t * (t - 2.0) / 2.0,
        (t + 1.0) * t * (t - 1.0) / 6.0,
    )


def halves(values):
    upper = values.astype(jnp.bfloat16)
    return upper, (values - upper.astype(jnp.float32)).astype(jnp.bfloat16)


def wide(row):
    return jnp.broadcast_to(row, (SUB, BLK))


def lanes_at(values, index):
    return jnp.take_along_axis(values, index, axis=1, mode="promise_in_bounds")


def row_of(values, row):
    index = jnp.full((SUB, BLK), row, jnp.int32)
    return jnp.take_along_axis(values, index, axis=0, mode="promise_in_bounds")


def cubic_limited(values, anchor, weights):
    before = lanes_at(values, anchor - 1)
    here = lanes_at(values, anchor)
    after = lanes_at(values, anchor + 1)
    beyond = lanes_at(values, anchor + 2)
    mixed = weights[0] * before + weights[1] * here + weights[2] * after + weights[3] * beyond
    return jnp.minimum(jnp.maximum(mixed, jnp.minimum(here, after)), jnp.maximum(here, after))


def lanes(block):
    return pl.ds(pl.multiple_of(block * BLK, BLK), BLK)


def kernel(
    n_lat, n_lon, src_h, cut_h, trc_h, off_h, frac_h, mat_h, twd_h, out,
    src_s, cut_s, trc, off, frac, mat, twd,
    mid, side_0, side_1, side_2, side_3, ring, ids, ids_out, fracs, ids_s, coef, anch, damp, lim, spec, done, back,
    halo_send, halo_recv, pol_send, pol_recv, idx_send, idx_recv, frc_send, frc_recv,
    ret_send, ret_recv, loc_sem,
):
    sides = (side_0, side_1, side_2, side_3)
    channels, rows, cells = trc.shape
    nb = cells // BLK
    groups = channels // SUB
    shares = n_lon // groups
    work_rows = PROWS // shares
    part_rows = work_rows // PARTS
    tall = part_rows * SUB
    lat, lon = lax.axis_index("lat"), lax.axis_index("lon")
    first_row = lat * rows
    first_block = lon * nb
    right, left = lax.rem(lon + 1, n_lon), lax.rem(lon + n_lon - 1, n_lon)
    down, up = lax.rem(lat + 1, n_lat), lax.rem(lat + n_lat - 1, n_lat)
    polar = (lat == 0) | (lat == n_lat - 1)
    slab = jnp.where(lat == 0, 0, rows - PROWS)
    worker = (lat == 2) | (lat == n_lat - 3)
    northern = lat < n_lat // 2
    mate = jnp.where(northern, 2 - lat, 2 * n_lat - 4 - lat)
    pole = jnp.where(northern, 0, 1)
    peers = [lax.rem(lon + d, n_lon) for d in range(n_lon)]

    edges = sorted({0, nb - 1})
    middle = list(range(1, nb - 1))

    def local(src, dst, sem):
        return pltpu.make_async_copy(src, dst, loc_sem.at[sem])

    def block_span(first_block_in, count):
        return pl.ds(first_block_in * BLK, count * BLK)

    loads = [
        local(trc_h.at[:, :, block_span(b, 1)], trc.at[:, :, block_span(b, 1)], n)
        for n, b in enumerate(edges)
    ]
    small = [local(off_h, off, 2), local(frac_h, frac, 3), local(src_h, src_s, 4)]
    tables = [local(cut_h, cut_s, 5), local(mat_h, mat, 6), local(twd_h, twd, 7)]
    for copy in loads:
        copy.start()
    centre = []
    if middle:
        span = block_span(1, len(middle))
        centre = [local(trc_h.at[:, :, span], trc.at[:, :, span], 8)]
    for copy in small + centre:
        copy.start()

    @pl.when(worker)
    def _():
        for copy in tables:
            copy.start()

    barrier = pltpu.get_barrier_semaphore()
    for device in ((lat, left), (lat, right), (up, lon), (down, lon)):
        pl.semaphore_signal(barrier, inc=1, device_id=device, device_id_type=MESH)

    @pl.when(polar | worker)
    def _():
        for peer in peers:
            pl.semaphore_signal(barrier, inc=1, device_id=(mate, peer), device_id_type=MESH)

    def turn(blocks, row_groups, skip_pole):
        @pl.loop(0, groups * len(row_groups))
        def _(step):
            ch = pl.multiple_of(lax.rem(step, groups) * SUB, SUB)
            index = lax.div(step, groups)
            row = pl.multiple_of(index * SUB if len(row_groups) > 1 else row_groups[0], SUB)

            def move():
                for b in blocks:
                    tile = trc[pl.ds(ch, SUB), pl.ds(row, SUB), b * BLK : (b + 1) * BLK]
                    mid[pl.ds(HL + row, SUB), b, pl.ds(ch, SUB), :] = jnp.swapaxes(tile, 0, 1)

            if skip_pole:
                pl.when(jnp.logical_not(polar & (row == slab)))(move)
            else:
                move()

    every = range(rows // SUB)
    for copy in loads:
        copy.wait()

    @pl.when(polar)
    def _():
        for copy in centre:
            copy.wait()
        turn(edges + middle, [slab], False)

    @pl.when(jnp.logical_not(polar))
    def _():
        turn(edges, every, False)

    pl.semaphore_wait(barrier, jnp.where(polar | worker, 4 + n_lon, 4))

    def group_of(place):
        return pl.multiple_of(lax.rem(place, groups) * SUB, SUB)

    def span_of(place):
        return pl.ds(place * nb, nb)

    def remote(src, dst, send, recv, device):
        return pltpu.make_async_remote_copy(
            src_ref=src, dst_ref=dst, send_sem=send, recv_sem=recv,
            device_id=device, device_id_type=MESH,
        )

    slab_at = pl.ds(pl.multiple_of(slab, SUB), PROWS)
    own = span_of(lon)
    ring_copies, back_copies = [], []
    for d, peer in enumerate(peers):
        ring_copies += [
            remote(ids_out, ids.at[lon], idx_send.at[d], idx_recv.at[d], (mate, peer)),
            remote(frac.at[slab_at], fracs.at[lon], frc_send.at[d], frc_recv.at[d], (mate, peer)),
            remote(
                mid.at[pl.ds(HL + slab, PROWS), :, pl.ds(group_of(peer), SUB), :],
                ring.at[:, own],
                pol_send.at[d], pol_recv.at[d], (mate, peer),
            ),
        ]

    for part in range(PARTS):
        for d, peer in enumerate(peers):
            to_row = lax.div(lon, groups) * work_rows + part * part_rows
            back_copies.append(
                remote(
                    done.at[pl.ds(part * part_rows, part_rows), span_of(peer)],
                    back.at[pl.ds(to_row, part_rows), :, pl.ds(group_of(lon), SUB), :],
                    ret_send.at[part * n_lon + d], ret_recv.at[part * n_lon + d], (mate, peer),
                )
            )

    first, last = 0, nb - 1
    top, bottom = pl.ds(HL, HL), pl.ds(rows, HL)
    over, under = pl.ds(0, HL), pl.ds(HL + rows, HL)
    inner = pl.ds(2 * HL, rows - 2 * HL)
    some = pl.ds(jnp.where(lat == 0, PROWS, 2 * HL), rows - PROWS)
    has_up, has_down = lat > 0, lat < n_lat - 1
    counter = iter(range(100))

    def halo(src, dst, device):
        n = next(counter)
        return remote(src, dst, halo_send.at[n], halo_recv.at[n], device)

    lat_halos = [
        (has_down, has_up, halo(mid.at[bottom], mid.at[over], (down, lon))),
        (has_up, has_down, halo(mid.at[top], mid.at[under], (up, lon))),
    ]
    lon_halos, rims, passed = [], [], []
    for g in range(groups):
        chans, side = pl.ds(g * SUB, SUB), sides[g]
        copies = []
        for to, block, half in ((right, last, 0), (left, first, 1)):
            n = next(counter)
            for span, when in ((inner, jnp.logical_not(polar)), (some, polar)):
                copies.append((when, when, remote(
                    mid.at[span, block, chans], side.at[half, span],
                    halo_send.at[n], halo_recv.at[n], (lat, to),
                )))
            for span, when in ((top, has_up), (bottom, has_down)):
                rims.append((when, when, halo(
                    mid.at[span, block, chans], side.at[half, span], (lat, to))))
            forward = [
                (has_down, has_up, halo(side.at[half, bottom], side.at[half, over], (down, lon))),
                (has_up, has_down, halo(side.at[half, top], side.at[half, under], (up, lon))),
            ]
            passed += forward
            copies += forward
        lon_halos.append(copies)

    def gated(condition, action):
        @pl.when(condition)
        def _():
            action()

    for copy in small:
        copy.wait()

    @pl.when(polar)
    def _():
        ids_out[0:PROWS] = off[slab_at]
        placed = jnp.zeros((PROWS, BLK), jnp.int32)
        row_ids = lax.broadcasted_iota(jnp.int32, (PROWS, BLK), 0)
        lane_ids = lax.broadcasted_iota(jnp.int32, (PROWS, BLK), 1)
        for j in range(PROWS):
            for b in range(nb):
                placed = jnp.where((row_ids == j) & (lane_ids == b), src_s[b, slab + j], placed)
        ids_out[PROWS : 2 * PROWS, 0:BLK] = placed
        if nb > 1:
            ids_out[PROWS : 2 * PROWS, BLK:] = jnp.zeros((PROWS, cells - BLK), jnp.int32)
        for copy in ring_copies:
            copy.start()
        turn(edges + middle, every, True)

    def send_lon(chosen):
        for g in chosen:
            for sends, _, copy in lon_halos[g]:
                if all(copy is not other for _, _, other in passed):
                    gated(sends, copy.start)

    for sends, _, copy in rims:
        gated(sends, copy.start)
    send_lon(range(EARLY))

    @pl.when(jnp.logical_not(polar))
    def _():
        for copy in centre:
            copy.wait()
        if middle:
            turn(middle, every, False)

    for sends, _, copy in lat_halos:
        gated(sends, copy.start)

    def tile(group, b, edge, chosen):
        row = pl.multiple_of(group * SUB, SUB)
        at = lanes(b)
        weights = weights_of(frac[pl.ds(row, SUB), at])
        anchors = off[pl.ds(row, SUB), at]
        results = {g: [] for g in chosen}
        for j in range(SUB):
            block_id = src_s[b, row + j]
            source_row = lax.div(block_id, NBLK) - first_row + HL
            source_row = jnp.clip(source_row, 0, rows + 2 * HL - 1)
            place = lax.rem(lax.rem(block_id, NBLK) - first_block + 1 + NBLK, NBLK)
            near = jnp.clip(place - 1, 0, nb - 1)
            far = jnp.minimum(place, 1)
            spot = jnp.full((SUB, BLK), place, jnp.int32)
            inside = (spot >= 1) & (spot <= nb)
            anchor = wide(anchors[j : j + 1])
            factors = [wide(w[j : j + 1]) for w in weights]
            for g in chosen:
                values = mid[source_row, near, pl.ds(g * SUB, SUB), :]
                if edge:
                    values = jnp.where(inside, values, sides[g][far, source_row])
                results[g].append(cubic_limited(values, anchor, factors))
        for g in chosen:
            out[g * SUB : (g + 1) * SUB, pl.ds(row, SUB), at] = jnp.swapaxes(
                jnp.stack(results[g]), 0, 1
            )

    tiles = rows // SUB

    def sweep(blocks, edge, chosen):
        count = len(blocks)
        if not count:
            return
        start, stride = blocks[0], (blocks[1] - blocks[0] if count > 1 else 1)

        @pl.loop(0, tiles * count)
        def _(step):
            group = lax.div(step, count)
            at_pole = ((lat == 0) & (group == 0)) | ((lat == n_lat - 1) & (group == tiles - 1))

            @pl.when(jnp.logical_not(at_pole))
            def _():
                tile(group, start + stride * lax.rem(step, count), edge, chosen)

    for _, receives, copy in rims:
        gated(receives, copy.wait_recv)
    for sends, _, copy in passed:
        gated(sends, copy.start)

    def inner_tiles():
        for _, receives, copy in lat_halos:
            gated(receives, copy.wait_recv)
        sweep(middle, False, range(groups))

    @pl.when(jnp.logical_not(worker))
    def _():
        inner_tiles()

    @pl.when(worker)
    def _():
        for copy in tables:
            copy.wait()
        for n in range(0, len(ring_copies), 3):
            ring_copies[n].wait_recv()
            ring_copies[n + 1].wait_recv()
        fetch = pltpu.make_async_copy(
            ids.at[:, pl.ds(PROWS, PROWS), pl.ds(0, BLK)], ids_s, loc_sem.at[9]
        )
        fetch.start()
        row_base = lax.div(lon, groups) * work_rows
        slab_global = jnp.where(northern, 0, n_lat * rows - PROWS)

        @pl.loop(0, work_rows)
        def _(j):
            jw = row_base + j
            for b in range(NBLK):
                q, at = b // nb, pl.ds(b % nb * BLK, BLK)
                for n, weight in enumerate(weights_of(row_of(fracs[q, :, at], jw))):
                    coef[j, b, n] = weight
                anch[j, b] = row_of(ids[q, 0:PROWS, at], jw)
            kappa = cut_s[pole, jw].astype(jnp.float32)
            for k in range(HALF):
                wave = k + NBLK * lax.broadcasted_iota(jnp.int32, (SUB, BLK), 1)
                wave = jnp.minimum(wave, NLON - wave)
                kept = (wave >= 1) & (wave < NLON // 2)
                damping = 1.0 - kappa / jnp.maximum(wave, 1).astype(jnp.float32)
                damp[j, k] = jnp.where(kept, jnp.maximum(damping, 0.0), 0.0) * (1.0 / NLON)

        inner_tiles()
        fetch.wait()
        for n in range(2, len(ring_copies), 3):
            ring_copies[n].wait_recv()
        send_lon(range(EARLY, groups))

        def transform():
            upper, lower = halves(spec[...])
            mat_upper, mat_lower = halves(mat[...])
            product = functools.partial(jnp.dot, preferred_element_type=jnp.float32)
            spec[...] = product(upper, mat_upper) + (
                product(lower, mat_upper) + product(upper, mat_lower)
            )

        for part in range(PARTS):

            @pl.loop(0, part_rows)
            def _(step):
                j = part * part_rows + step
                jw = row_base + j
                band = []
                for b in range(NBLK):
                    q, bb = b // nb, b % nb
                    block_id = ids_s[q, jw, bb]
                    source_row = jnp.clip(lax.div(block_id, NBLK) - slab_global, 0, PROWS - 1)
                    values = ring[source_row, lax.rem(block_id, NBLK)]
                    limited = cubic_limited(values, anch[j, b], [coef[j, b, n] for n in range(4)])
                    lim[j, b] = limited
                    band.append((limited, None))
                waves = fourier(band, -1)
                for k in range(HALF):
                    re, im = waves[k]
                    cosine, sine = wide(twd[0, k : k + 1, :]), wide(twd[1, k : k + 1, :])
                    at = pl.ds(pl.multiple_of(k * tall + step * SUB, SUB), SUB)
                    if im is None:
                        spec[at, 0:BLK] = re * cosine
                        spec[at, BLK : 2 * BLK] = -re * sine
                    else:
                        spec[at, 0:BLK] = re * cosine + im * sine
                        spec[at, BLK : 2 * BLK] = im * cosine - re * sine

            transform()

            @pl.loop(0, part_rows)
            def _(step):
                j = part * part_rows + step
                for k in range(HALF):
                    damping = damp[j, k]
                    at = pl.ds(pl.multiple_of(k * tall + step * SUB, SUB), SUB)
                    spec[at, 0:BLK] = spec[at, 0:BLK] * damping
                    spec[at, BLK : 2 * BLK] = -spec[at, BLK : 2 * BLK] * damping

            transform()

            @pl.loop(0, part_rows)
            def _(step):
                j = part * part_rows + step
                waves = []
                for k in range(HALF):
                    at = pl.ds(pl.multiple_of(k * tall + step * SUB, SUB), SUB)
                    re, im = spec[at, 0:BLK], spec[at, BLK : 2 * BLK]
                    cosine, sine = wide(twd[0, k : k + 1, :]), wide(twd[1, k : k + 1, :])
                    real = re * cosine + im * sine
                    waves.append((real, None if k in (0, HALF - 1) else re * sine - im * cosine))
                for k in range(HALF, NBLK):
                    re, im = waves[NBLK - k]
                    waves.append((re, -im))
                removed = fourier(waves, 1)
                for b in range(NBLK):
                    done[j, b] = lim[j, b] - removed[b][0]

            for copy in back_copies[part * n_lon : (part + 1) * n_lon]:
                copy.start()

    for g, copies in enumerate(lon_halos):
        for _, receives, copy in copies:
            gated(receives, copy.wait_recv)
        if g == 0:

            @pl.when(jnp.logical_not(worker))
            def _():
                send_lon(range(EARLY, groups))

        sweep(edges, True, [g])

    @pl.when(polar)
    def _():
        for copy in back_copies:
            copy.wait_recv()

        @pl.loop(0, groups)
        def _(g):
            ch = pl.multiple_of(g * SUB, SUB)
            for b in range(nb):
                at = slice(b * BLK, (b + 1) * BLK)
                out[pl.ds(ch, SUB), slab_at, at] = jnp.swapaxes(back[:, b, pl.ds(ch, SUB), :], 0, 1)

        for copy in ring_copies:
            copy.wait_send()

    @pl.when(worker)
    def _():
        for copy in back_copies:
            copy.wait_send()

    for sends, _, copy in lat_halos + rims + sum(lon_halos, []):
        gated(sends, copy.wait_send)


def body(n_lat, n_lon, tracer, source, offset, fraction, cutoffs):
    channels, rows, cells = tracer.shape
    shares = n_lon // (channels // SUB)
    work_rows = PROWS // shares
    matrix, twiddle = dft_tables()
    operands = (
        source.T, cutoffs, tracer, offset, fraction, jnp.asarray(matrix), jnp.asarray(twiddle)
    )
    dma = pltpu.SemaphoreType.DMA
    vmem = pl.BlockSpec(memory_space=pltpu.VMEM)
    return pl.pallas_call(
        functools.partial(kernel, n_lat, n_lon),
        out_shape=jax.ShapeDtypeStruct(tracer.shape, jnp.float32),
        in_specs=[pl.BlockSpec(memory_space=pltpu.HBM)] * 7,
        out_specs=vmem,
        scratch_shapes=[
            pltpu.SMEM(source.shape[::-1], jnp.int32),
            pltpu.SMEM(cutoffs.shape, jnp.int32),
            pltpu.VMEM(tracer.shape, jnp.float32),
            pltpu.VMEM(offset.shape, jnp.int32),
            pltpu.VMEM(fraction.shape, jnp.float32),
            pltpu.VMEM(matrix.shape, jnp.float32),
            pltpu.VMEM(twiddle.shape, jnp.float32),
            pltpu.VMEM((rows + 2 * HL, cells // BLK, channels, BLK), jnp.float32),
        ] + [pltpu.VMEM((2, rows + 2 * HL, SUB, BLK), jnp.float32)] * 4 + [
            pltpu.VMEM((PROWS, NBLK, SUB, BLK), jnp.float32),
            pltpu.VMEM((n_lon, 2 * PROWS, cells), jnp.int32),
            pltpu.VMEM((2 * PROWS, cells), jnp.int32),
            pltpu.VMEM((n_lon, PROWS, cells), jnp.float32),
            pltpu.SMEM((n_lon, PROWS, BLK), jnp.int32),
            pltpu.VMEM((work_rows, NBLK, 4, SUB, BLK), jnp.float32),
            pltpu.VMEM((work_rows, NBLK, SUB, BLK), jnp.int32),
            pltpu.VMEM((work_rows, HALF, SUB, BLK), jnp.float32),
            pltpu.VMEM((work_rows, NBLK, SUB, BLK), jnp.float32),
            pltpu.VMEM((HALF * work_rows // PARTS * SUB, 2 * BLK), jnp.float32),
            pltpu.VMEM((work_rows, NBLK, SUB, BLK), jnp.float32),
            pltpu.VMEM((PROWS, cells // BLK, channels, BLK), jnp.float32),
            dma((42,)), dma((42,)),
        ] + [dma((n_lon,))] * 6 + [dma((PARTS * n_lon,))] * 2 + [dma((10,))],
        compiler_params=pltpu.CompilerParams(
            collective_id=0, has_side_effects=True, vmem_limit_bytes=VMEM_LIMIT
        ),
        cost_estimate=pl.CostEstimate(flops=10**9, bytes_accessed=5 * 10**6, transcendentals=0),
    )(*(pltpu.with_memory_space_constraint(value, pltpu.HBM) for value in operands))


def solution(mesh):
    placed = (P(None, "lat", "lon"), P("lat", "lon"), P("lat", "lon"), P("lat", "lon"), P())
    step = functools.partial(body, mesh.shape["lat"], mesh.shape["lon"])
    return jax.shard_map(
        step, mesh=mesh, in_specs=placed, out_specs=P(None, "lat", "lon"), check_vma=False
    )
```

```python
import functools
import math

import jax
import jax.numpy as jnp
import numpy as np
from jax import lax
from jax.experimental import pallas as pl
from jax.experimental.pallas import tpu as pltpu
from jax.sharding import PartitionSpec as P

NLON = 2048
BLK = 128
HL = 2
PROWS = 8
NBLK = NLON // BLK
SUB = 8
HALF = NBLK // 2 + 1
PARTS = 2
PIECES = 4
MESH = pl.DeviceIdType.MESH
VMEM_LIMIT = 48 * 2**20


def dft_tables():
    lanes = np.arange(BLK)
    angles = 2.0 * math.pi * (np.outer(lanes, lanes) % BLK) / BLK
    cosines, sines = np.cos(angles), np.sin(angles)
    matrix = np.block([[cosines, -sines], [sines, cosines]])
    turns = 2.0 * math.pi * np.outer(np.arange(NBLK), lanes) / NLON
    twiddle = np.stack([np.cos(turns), np.sin(turns)])
    return matrix.astype(np.float32), twiddle.astype(np.float32)


def add(left, right):
    if left is None:
        return right
    return left if right is None else left + right


def sub(left, right):
    if right is None:
        return left
    return -right if left is None else left - right


def scaled(value, factor):
    return None if value is None or factor == 0.0 else value * factor


def turned(value, cosine, sine):
    re, im = value
    cosine, sine = (0.0 if abs(v) < 1e-12 else v for v in (cosine, sine))
    if sine == 0.0 and cosine == 1.0:
        return value
    if cosine == 0.0 and abs(sine) == 1.0:
        if sine > 0:
            return (None if im is None else -im), re
        return im, (None if re is None else -re)
    return sub(scaled(re, cosine), scaled(im, sine)), add(scaled(re, sine), scaled(im, cosine))


def fourier(values, sign):
    count = len(values)
    if count == 1:
        return values
    even, odd = fourier(values[::2], sign), fourier(values[1::2], sign)
    low, high = [], []
    for k in range(count // 2):
        angle = sign * 2.0 * math.pi * k / count
        re, im = turned(odd[k], math.cos(angle), math.sin(angle))
        low.append((add(even[k][0], re), add(even[k][1], im)))
        high.append((sub(even[k][0], re), sub(even[k][1], im)))
    return low + high


def weights_of(t):
    return (
        -t * (t - 1.0) * (t - 2.0) / 6.0,
        (t + 1.0) * (t - 1.0) * (t - 2.0) / 2.0,
        -(t + 1.0) * t * (t - 2.0) / 2.0,
        (t + 1.0) * t * (t - 1.0) / 6.0,
    )


def halves(values):
    upper = values.astype(jnp.bfloat16)
    return upper, (values - upper.astype(jnp.float32)).astype(jnp.bfloat16)


def wide(row):
    return jnp.broadcast_to(row, (SUB, BLK))


def lanes_at(values, index):
    return jnp.take_along_axis(values, index, axis=1, mode="promise_in_bounds")


def row_of(values, row):
    index = jnp.full((SUB, BLK), row, jnp.int32)
    return jnp.take_along_axis(values, index, axis=0, mode="promise_in_bounds")


def cubic_limited(values, anchor, weights):
    before = lanes_at(values, anchor - 1)
    here = lanes_at(values, anchor)
    after = lanes_at(values, anchor + 1)
    beyond = lanes_at(values, anchor + 2)
    mixed = weights[0] * before + weights[1] * here + weights[2] * after + weights[3] * beyond
    return jnp.minimum(jnp.maximum(mixed, jnp.minimum(here, after)), jnp.maximum(here, after))


def lanes(block):
    return pl.ds(pl.multiple_of(block * BLK, BLK), BLK)


def kernel(
    n_lat, n_lon, src_h, cut_h, trc_h, off_h, frac_h, mat_h, twd_h, out,
    src_s, cut_s, trc, off, frac, mat, twd,
    mid, side_0, side_1, side_2, side_3, ring, ids, ids_out, fracs, ids_s, coef, anch, damp, lim, spec, done, back,
    halo_send, halo_recv, pol_send, pol_recv, idx_send, idx_recv, frc_send, frc_recv,
    ret_send, ret_recv, loc_sem,
):
    sides = (side_0, side_1, side_2, side_3)
    channels, rows, cells = trc.shape
    nb = cells // BLK
    groups = channels // SUB
    shares = n_lon // groups
    work_rows = PROWS // shares
    part_rows = work_rows // PARTS
    tall = part_rows * SUB
    lat, lon = lax.axis_index("lat"), lax.axis_index("lon")
    first_row = lat * rows
    first_block = lon * nb
    right, left = lax.rem(lon + 1, n_lon), lax.rem(lon + n_lon - 1, n_lon)
    down, up = lax.rem(lat + 1, n_lat), lax.rem(lat + n_lat - 1, n_lat)
    polar = (lat == 0) | (lat == n_lat - 1)
    slab = jnp.where(lat == 0, 0, rows - PROWS)
    worker = (lat == 2) | (lat == n_lat - 3)
    northern = lat < n_lat // 2
    mate = jnp.where(northern, 2 - lat, 2 * n_lat - 4 - lat)
    pole = jnp.where(northern, 0, 1)
    peers = [lax.rem(lon + d, n_lon) for d in range(n_lon)]

    edges = sorted({0, nb - 1})
    middle = list(range(1, nb - 1))

    def local(src, dst, sem):
        return pltpu.make_async_copy(src, dst, loc_sem.at[sem])

    def block_span(first_block_in, count):
        return pl.ds(first_block_in * BLK, count * BLK)

    loads = [
        local(trc_h.at[:, :, block_span(b, 1)], trc.at[:, :, block_span(b, 1)], n)
        for n, b in enumerate(edges)
    ]
    small = [local(off_h, off, 2), local(frac_h, frac, 3), local(src_h, src_s, 4)]
    tables = [local(cut_h, cut_s, 5), local(mat_h, mat, 6), local(twd_h, twd, 7)]
    for copy in loads:
        copy.start()
    centre = []
    if middle:
        span = block_span(1, len(middle))
        centre = [local(trc_h.at[:, :, span], trc.at[:, :, span], 8)]
    for copy in small + centre:
        copy.start()

    @pl.when(worker)
    def _():
        for copy in tables:
            copy.start()

    barrier = pltpu.get_barrier_semaphore()
    for device in ((lat, left), (lat, right), (up, lon), (down, lon)):
        pl.semaphore_signal(barrier, inc=1, device_id=device, device_id_type=MESH)

    @pl.when(polar | worker)
    def _():
        for peer in peers:
            pl.semaphore_signal(barrier, inc=1, device_id=(mate, peer), device_id_type=MESH)

    def turn(blocks, row_groups, skip_pole):
        @pl.loop(0, groups * len(row_groups))
        def _(step):
            ch = pl.multiple_of(lax.rem(step, groups) * SUB, SUB)
            index = lax.div(step, groups)
            row = pl.multiple_of(index * SUB if len(row_groups) > 1 else row_groups[0], SUB)

            def move():
                for b in blocks:
                    tile = trc[pl.ds(ch, SUB), pl.ds(row, SUB), b * BLK : (b + 1) * BLK]
                    mid[pl.ds(HL + row, SUB), b, pl.ds(ch, SUB), :] = jnp.swapaxes(tile, 0, 1)

            if skip_pole:
                pl.when(jnp.logical_not(polar & (row == slab)))(move)
            else:
                move()

    every = range(rows // SUB)
    for copy in loads:
        copy.wait()

    @pl.when(polar)
    def _():
        for copy in centre:
            copy.wait()
        turn(edges + middle, [slab], False)

    @pl.when(jnp.logical_not(polar))
    def _():
        turn(edges, every, False)

    pl.semaphore_wait(barrier, jnp.where(polar | worker, 4 + n_lon, 4))

    def group_of(place):
        return pl.multiple_of(lax.rem(place, groups) * SUB, SUB)

    def span_of(place):
        return pl.ds(place * nb, nb)

    def remote(src, dst, send, recv, device):
        return pltpu.make_async_remote_copy(
            src_ref=src, dst_ref=dst, send_sem=send, recv_sem=recv,
            device_id=device, device_id_type=MESH,
        )

    slab_at = pl.ds(pl.multiple_of(slab, SUB), PROWS)
    own = span_of(lon)
    ring_copies, back_copies = [], []
    for d, peer in enumerate(peers):
        ring_copies += [
            remote(ids_out, ids.at[lon], idx_send.at[d], idx_recv.at[d], (mate, peer)),
            remote(frac.at[slab_at], fracs.at[lon], frc_send.at[d], frc_recv.at[d], (mate, peer)),
        ]

    piece_rows = PROWS // PIECES
    for piece in range(PIECES):
        for d, peer in enumerate(peers):
            ring_copies.append(
                remote(
                    mid.at[
                        pl.ds(HL + slab + piece * piece_rows, piece_rows), :,
                        pl.ds(group_of(peer), SUB), :,
                    ],
                    ring.at[pl.ds(piece * piece_rows, piece_rows), own],
                    pol_send.at[piece * n_lon + d], pol_recv.at[piece * n_lon + d], (mate, peer),
                )
            )

    for part in range(PARTS):
        for d, peer in enumerate(peers):
            to_row = lax.div(lon, groups) * work_rows + part * part_rows
            back_copies.append(
                remote(
                    done.at[pl.ds(part * part_rows, part_rows), span_of(peer)],
                    back.at[pl.ds(to_row, part_rows), :, pl.ds(group_of(lon), SUB), :],
                    ret_send.at[part * n_lon + d], ret_recv.at[part * n_lon + d], (mate, peer),
                )
            )

    first, last = 0, nb - 1
    top, bottom = pl.ds(HL, HL), pl.ds(rows, HL)
    over, under = pl.ds(0, HL), pl.ds(HL + rows, HL)
    inner = pl.ds(2 * HL, rows - 2 * HL)
    some = pl.ds(jnp.where(lat == 0, PROWS, 2 * HL), rows - PROWS)
    has_up, has_down = lat > 0, lat < n_lat - 1
    counter = iter(range(100))

    def halo(src, dst, device):
        n = next(counter)
        return remote(src, dst, halo_send.at[n], halo_recv.at[n], device)

    lat_halos = [
        (has_down, has_up, halo(mid.at[bottom], mid.at[over], (down, lon))),
        (has_up, has_down, halo(mid.at[top], mid.at[under], (up, lon))),
    ]
    lon_halos, rims, passed = [], [], []
    for g in range(groups):
        chans, side = pl.ds(g * SUB, SUB), sides[g]
        copies = []
        for to, block, half in ((right, last, 0), (left, first, 1)):
            n = next(counter)
            for span, when in ((inner, jnp.logical_not(polar)), (some, polar)):
                copies.append((when, when, remote(
                    mid.at[span, block, chans], side.at[half, span],
                    halo_send.at[n], halo_recv.at[n], (lat, to),
                )))
            for span, when in ((top, has_up), (bottom, has_down)):
                rims.append((when, when, halo(
                    mid.at[span, block, chans], side.at[half, span], (lat, to))))
            forward = [
                (has_down, has_up, halo(side.at[half, bottom], side.at[half, over], (down, lon))),
                (has_up, has_down, halo(side.at[half, top], side.at[half, under], (up, lon))),
            ]
            passed += forward
            copies += forward
        lon_halos.append(copies)

    def gated(condition, action):
        @pl.when(condition)
        def _():
            action()

    for copy in small:
        copy.wait()

    @pl.when(polar)
    def _():
        ids_out[0:PROWS] = off[slab_at]
        placed = jnp.zeros((PROWS, BLK), jnp.int32)
        row_ids = lax.broadcasted_iota(jnp.int32, (PROWS, BLK), 0)
        lane_ids = lax.broadcasted_iota(jnp.int32, (PROWS, BLK), 1)
        for j in range(PROWS):
            for b in range(nb):
                placed = jnp.where((row_ids == j) & (lane_ids == b), src_s[b, slab + j], placed)
        ids_out[PROWS : 2 * PROWS, 0:BLK] = placed
        if nb > 1:
            ids_out[PROWS : 2 * PROWS, BLK:] = jnp.zeros((PROWS, cells - BLK), jnp.int32)
        for copy in ring_copies:
            copy.start()
        turn(edges + middle, every, True)

    def send_lon(chosen):
        for g in chosen:
            for sends, _, copy in lon_halos[g]:
                if all(copy is not other for _, _, other in passed):
                    gated(sends, copy.start)

    for sends, _, copy in rims:
        gated(sends, copy.start)
    send_lon(range(groups))

    @pl.when(jnp.logical_not(polar))
    def _():
        for copy in centre:
            copy.wait()
        if middle:
            turn(middle, every, False)

    for sends, _, copy in lat_halos:
        gated(sends, copy.start)

    def tile(group, b, edge, chosen):
        row = pl.multiple_of(group * SUB, SUB)
        at = lanes(b)
        weights = weights_of(frac[pl.ds(row, SUB), at])
        anchors = off[pl.ds(row, SUB), at]
        results = {g: [] for g in chosen}
        for j in range(SUB):
            block_id = src_s[b, row + j]
            source_row = lax.div(block_id, NBLK) - first_row + HL
            source_row = jnp.clip(source_row, 0, rows + 2 * HL - 1)
            place = lax.rem(lax.rem(block_id, NBLK) - first_block + 1 + NBLK, NBLK)
            near = jnp.clip(place - 1, 0, nb - 1)
            far = jnp.minimum(place, 1)
            spot = jnp.full((SUB, BLK), place, jnp.int32)
            inside = (spot >= 1) & (spot <= nb)
            anchor = wide(anchors[j : j + 1])
            factors = [wide(w[j : j + 1]) for w in weights]
            for g in chosen:
                values = mid[source_row, near, pl.ds(g * SUB, SUB), :]
                if edge:
                    values = jnp.where(inside, values, sides[g][far, source_row])
                results[g].append(cubic_limited(values, anchor, factors))
        for g in chosen:
            out[g * SUB : (g + 1) * SUB, pl.ds(row, SUB), at] = jnp.swapaxes(
                jnp.stack(results[g]), 0, 1
            )

    tiles = rows // SUB

    def sweep(blocks, edge, chosen):
        count = len(blocks)
        if not count:
            return
        start, stride = blocks[0], (blocks[1] - blocks[0] if count > 1 else 1)

        @pl.loop(0, tiles * count)
        def _(step):
            group = lax.div(step, count)
            at_pole = ((lat == 0) & (group == 0)) | ((lat == n_lat - 1) & (group == tiles - 1))

            @pl.when(jnp.logical_not(at_pole))
            def _():
                tile(group, start + stride * lax.rem(step, count), edge, chosen)

    for _, receives, copy in rims:
        gated(receives, copy.wait_recv)
    for sends, _, copy in passed:
        gated(sends, copy.start)

    def inner_tiles():
        for _, receives, copy in lat_halos:
            gated(receives, copy.wait_recv)
        sweep(middle, False, range(groups))

    @pl.when(jnp.logical_not(worker))
    def _():
        inner_tiles()

    @pl.when(worker)
    def _():
        for copy in tables:
            copy.wait()
        for copy in ring_copies[: 2 * n_lon]:
            copy.wait_recv()
        fetch = pltpu.make_async_copy(
            ids.at[:, pl.ds(PROWS, PROWS), pl.ds(0, BLK)], ids_s, loc_sem.at[9]
        )
        fetch.start()
        row_base = lax.div(lon, groups) * work_rows
        slab_global = jnp.where(northern, 0, n_lat * rows - PROWS)

        @pl.loop(0, work_rows)
        def _(j):
            jw = row_base + j
            for b in range(NBLK):
                q, at = b // nb, pl.ds(b % nb * BLK, BLK)
                for n, weight in enumerate(weights_of(row_of(fracs[q, :, at], jw))):
                    coef[j, b, n] = weight
                anch[j, b] = row_of(ids[q, 0:PROWS, at], jw)
            kappa = cut_s[pole, jw].astype(jnp.float32)
            for k in range(HALF):
                wave = k + NBLK * lax.broadcasted_iota(jnp.int32, (SUB, BLK), 1)
                wave = jnp.minimum(wave, NLON - wave)
                kept = (wave >= 1) & (wave < NLON // 2)
                damping = 1.0 - kappa / jnp.maximum(wave, 1).astype(jnp.float32)
                damp[j, k] = jnp.where(kept, jnp.maximum(damping, 0.0), 0.0) * (1.0 / NLON)

        inner_tiles()
        fetch.wait()
        for copy in ring_copies[2 * n_lon :]:
            copy.wait_recv()

        def transform():
            upper, lower = halves(spec[...])
            mat_upper, mat_lower = halves(mat[...])
            product = functools.partial(jnp.dot, preferred_element_type=jnp.float32)
            spec[...] = product(upper, mat_upper) + (
                product(lower, mat_upper) + product(upper, mat_lower)
            )

        for part in range(PARTS):

            @pl.loop(0, part_rows)
            def _(step):
                j = part * part_rows + step
                jw = row_base + j
                band = []
                for b in range(NBLK):
                    q, bb = b // nb, b % nb
                    block_id = ids_s[q, jw, bb]
                    source_row = jnp.clip(lax.div(block_id, NBLK) - slab_global, 0, PROWS - 1)
                    values = ring[source_row, lax.rem(block_id, NBLK)]
                    limited = cubic_limited(values, anch[j, b], [coef[j, b, n] for n in range(4)])
                    lim[j, b] = limited
                    band.append((limited, None))
                waves = fourier(band, -1)
                for k in range(HALF):
                    re, im = waves[k]
                    cosine, sine = wide(twd[0, k : k + 1, :]), wide(twd[1, k : k + 1, :])
                    at = pl.ds(pl.multiple_of(k * tall + step * SUB, SUB), SUB)
                    if im is None:
                        spec[at, 0:BLK] = re * cosine
                        spec[at, BLK : 2 * BLK] = -re * sine
                    else:
                        spec[at, 0:BLK] = re * cosine + im * sine
                        spec[at, BLK : 2 * BLK] = im * cosine - re * sine

            transform()

            @pl.loop(0, part_rows)
            def _(step):
                j = part * part_rows + step
                for k in range(HALF):
                    damping = damp[j, k]
                    at = pl.ds(pl.multiple_of(k * tall + step * SUB, SUB), SUB)
                    spec[at, 0:BLK] = spec[at, 0:BLK] * damping
                    spec[at, BLK : 2 * BLK] = -spec[at, BLK : 2 * BLK] * damping

            transform()

            @pl.loop(0, part_rows)
            def _(step):
                j = part * part_rows + step
                waves = []
                for k in range(HALF):
                    at = pl.ds(pl.multiple_of(k * tall + step * SUB, SUB), SUB)
                    re, im = spec[at, 0:BLK], spec[at, BLK : 2 * BLK]
                    cosine, sine = wide(twd[0, k : k + 1, :]), wide(twd[1, k : k + 1, :])
                    real = re * cosine + im * sine
                    waves.append((real, None if k in (0, HALF - 1) else re * sine - im * cosine))
                for k in range(HALF, NBLK):
                    re, im = waves[NBLK - k]
                    waves.append((re, -im))
                removed = fourier(waves, 1)
                for b in range(NBLK):
                    done[j, b] = lim[j, b] - removed[b][0]

            for copy in back_copies[part * n_lon : (part + 1) * n_lon]:
                copy.start()

    for g, copies in enumerate(lon_halos):
        for _, receives, copy in copies:
            gated(receives, copy.wait_recv)
        sweep(edges, True, [g])

    @pl.when(polar)
    def _():
        for copy in back_copies:
            copy.wait_recv()

        @pl.loop(0, groups)
        def _(g):
            ch = pl.multiple_of(g * SUB, SUB)
            for b in range(nb):
                at = slice(b * BLK, (b + 1) * BLK)
                out[pl.ds(ch, SUB), slab_at, at] = jnp.swapaxes(back[:, b, pl.ds(ch, SUB), :], 0, 1)

        for copy in ring_copies:
            copy.wait_send()

    @pl.when(worker)
    def _():
        for copy in back_copies:
            copy.wait_send()

    for sends, _, copy in lat_halos + rims + sum(lon_halos, []):
        gated(sends, copy.wait_send)


def body(n_lat, n_lon, tracer, source, offset, fraction, cutoffs):
    channels, rows, cells = tracer.shape
    shares = n_lon // (channels // SUB)
    work_rows = PROWS // shares
    matrix, twiddle = dft_tables()
    operands = (
        source.T, cutoffs, tracer, offset, fraction, jnp.asarray(matrix), jnp.asarray(twiddle)
    )
    dma = pltpu.SemaphoreType.DMA
    vmem = pl.BlockSpec(memory_space=pltpu.VMEM)
    return pl.pallas_call(
        functools.partial(kernel, n_lat, n_lon),
        out_shape=jax.ShapeDtypeStruct(tracer.shape, jnp.float32),
        in_specs=[pl.BlockSpec(memory_space=pltpu.HBM)] * 7,
        out_specs=vmem,
        scratch_shapes=[
            pltpu.SMEM(source.shape[::-1], jnp.int32),
            pltpu.SMEM(cutoffs.shape, jnp.int32),
            pltpu.VMEM(tracer.shape, jnp.float32),
            pltpu.VMEM(offset.shape, jnp.int32),
            pltpu.VMEM(fraction.shape, jnp.float32),
            pltpu.VMEM(matrix.shape, jnp.float32),
            pltpu.VMEM(twiddle.shape, jnp.float32),
            pltpu.VMEM((rows + 2 * HL, cells // BLK, channels, BLK), jnp.float32),
        ] + [pltpu.VMEM((2, rows + 2 * HL, SUB, BLK), jnp.float32)] * 4 + [
            pltpu.VMEM((PROWS, NBLK, SUB, BLK), jnp.float32),
            pltpu.VMEM((n_lon, 2 * PROWS, cells), jnp.int32),
            pltpu.VMEM((2 * PROWS, cells), jnp.int32),
            pltpu.VMEM((n_lon, PROWS, cells), jnp.float32),
            pltpu.SMEM((n_lon, PROWS, BLK), jnp.int32),
            pltpu.VMEM((work_rows, NBLK, 4, SUB, BLK), jnp.float32),
            pltpu.VMEM((work_rows, NBLK, SUB, BLK), jnp.int32),
            pltpu.VMEM((work_rows, HALF, SUB, BLK), jnp.float32),
            pltpu.VMEM((work_rows, NBLK, SUB, BLK), jnp.float32),
            pltpu.VMEM((HALF * work_rows // PARTS * SUB, 2 * BLK), jnp.float32),
            pltpu.VMEM((work_rows, NBLK, SUB, BLK), jnp.float32),
            pltpu.VMEM((PROWS, cells // BLK, channels, BLK), jnp.float32),
            dma((42,)), dma((42,)),
        ] + [dma((PIECES * n_lon,))] * 2 + [dma((n_lon,))] * 4 + [dma((PARTS * n_lon,))] * 2 + [dma((10,))],
        compiler_params=pltpu.CompilerParams(
            collective_id=0, has_side_effects=True, vmem_limit_bytes=VMEM_LIMIT
        ),
        cost_estimate=pl.CostEstimate(flops=10**9, bytes_accessed=5 * 10**6, transcendentals=0),
    )(*(pltpu.with_memory_space_constraint(value, pltpu.HBM) for value in operands))


def solution(mesh):
    placed = (P(None, "lat", "lon"), P("lat", "lon"), P("lat", "lon"), P("lat", "lon"), P())
    step = functools.partial(body, mesh.shape["lat"], mesh.shape["lon"])
    return jax.shard_map(
        step, mesh=mesh, in_specs=placed, out_specs=P(None, "lat", "lon"), check_vma=False
    )
```
